128 devices in a mesh: member: 2 (over x_lo), tile: 64 (over z, y, x_hi, core).
Axes of the slice: x: 4 (x_hi: 2, x_lo: 2; x = x_hi * 2 + x_lo), y: 4, z: 4, core: 2. Of those that a mesh axis runs over, the one named last changes fastest.
Arguments:
- state: float32 [64, 12, 512, 512], P('member', None, 'tile'), may hold values from -6 to 6
- u_courant: float32 [4, 512, 512], P(None, 'tile'), may hold values from -0.5 to 0.5
- v_courant: float32 [4, 512, 512], P(None, 'tile'), may hold values from -0.5 to 0.5
- obs_index: int32 [512, 2048], P('tile'), may hold values from 0 to 6143
- obs_bin: int32 [512, 2048], P('tile'), may hold values from 0 to 31
- obs_value: float32 [512, 2048], P('tile'), may hold values from -8 to 8
- obs_weight: float32 [512, 2048], P('tile'), may hold values from 0.2 to 2
- obs_blocks: int32 [512], P('tile'), may hold values from 1 to 16, as said below
- loc_table: float32 [32], replicated, may hold values from 0.05 to 1
Outputs:
- analysis: float32 [64, 12, 512, 512], P('member', None, 'tile')
The draws below stay inside these ranges and needn't reach their ends.
Inputs may be any that keep to these rules, and one draw needn't show every extreme that they name: The live observations of a patch fill its first 128 * obs_blocks slots; the other slots are ignored.
All inputs are finite; a program needn't handle non-finite values.
Results may differ from the reference program's by a relative error of at most 0.0003.
Values sent between devices are 32-bit elements; how exact they have to be, the bound alone decides.
A program may use at most 128 MiB of HBM per device.

```python
import math
import jax
import jax.numpy as jnp
from jax import lax

K = 64
F = 3
L = 4
NY = 512
PATCH = 512
BLOCK = 128
MAXBLK = 16
LOCBINS = 32
SWEEPS = 8
NX = 512
C = 12
NPATCH = 512
MAXOBS = 2048


def draw_obs_blocks(key, part):
    key = jax.random.fold_in(key, 7)
    blocks = jax.random.randint(key, (NPATCH,), 1, MAXBLK + 1)
    return blocks.at[0].set(MAXBLK).astype(jnp.int32)


def plant(entries, stream_key, smallest, top_value):
    longest = entries.shape.index(max(entries.shape))
    spots = []
    for shift in (0, 1):
        where = [jax.random.randint(jax.random.fold_in(stream_key, axis), (), 0, length) for axis, length in enumerate(entries.shape)]
        where[longest] = (where[longest] + shift) % entries.shape[longest]
        spots.append(tuple(where))
    return entries.at[spots[0]].set(smallest).at[spots[1]].set(top_value)


def shard_levels(own_key, extent, shards, smallest, high):
    gain, own = 1.0, jax.random.fold_in(own_key, 6)
    for axis_at, parts in shards:
        draws = jnp.exp(jax.random.uniform(jax.random.fold_in(own, axis_at), (parts,), jnp.float32, smallest / len(shards), high / len(shards)))
        gain = gain * jnp.repeat(draws, extent[axis_at] // parts).reshape([-1 if axis == axis_at else 1 for axis in range(len(extent))])
    return gain


def scatter_about(own_key, shape, width, bound, split=(), kind=jnp.bfloat16):
    result = jax.random.normal(own_key, shape, jnp.float32) * width
    if len(split) > 0:
        result = shard_levels(own_key, shape, split, -0.22, 0.18) * result
    return jnp.clip(result, min=-bound, max=bound).astype(kind)


def setup_inputs(seed: int = 0) -> dict:
    key_of = jax.random.split(jax.random.key(seed), 10)
    state = scatter_about(key_of[0], (K, C, NX, NY), 1.0, 6.0, ((0, 2), (2, 64)), jnp.float32)
    u_courant = jnp.clip(jax.random.uniform(key_of[1], (L, NX, NY), jnp.float32, -0.5, 0.5) * shard_levels(key_of[1], (L, NX, NY), ((1, 64),), -0.4, 0.0), -0.5, 0.5)
    v_courant = jnp.clip(jax.random.uniform(key_of[2], (L, NX, NY), jnp.float32, -0.5, 0.5) * shard_levels(key_of[2], (L, NX, NY), ((1, 64),), -0.4, 0.0), -0.5, 0.5)
    obs_index = plant(jax.random.randint(key_of[3], (NPATCH, MAXOBS), 0, C * PATCH), jax.random.fold_in(key_of[3], 1), 0, (C * PATCH) - 1).astype(jnp.int32)
    obs_bin = plant(jax.random.randint(key_of[4], (NPATCH, MAXOBS), 0, LOCBINS), jax.random.fold_in(key_of[4], 1), 0, LOCBINS - 1).astype(jnp.int32)
    obs_value = scatter_about(key_of[5], (NPATCH, MAXOBS), 1.5, 8.0, ((0, 64),), jnp.float32)
    obs_weight = jnp.clip(jnp.exp(math.log(2.0) - 2.3025851 * jax.random.uniform(key_of[6], (NPATCH, MAXOBS), jnp.float32) ** shard_levels(key_of[6], (NPATCH, MAXOBS), ((0, 64),), -0.2, 0.2)), 0.2, 2.0)
    obs_blocks = draw_obs_blocks(jax.random.fold_in(key_of[9], 71), 0)
    loc_table = jnp.clip(jnp.exp(jax.random.uniform(key_of[8], (LOCBINS,), jnp.float32, math.log(0.05), math.log(1.0))), 0.05, 1.0)
    return {"state": state, "u_courant": u_courant, "v_courant": v_courant, "obs_index": obs_index, "obs_bin": obs_bin, "obs_value": obs_value, "obs_weight": obs_weight, "obs_blocks": obs_blocks, "loc_table": loc_table}


highest = lax.Precision.HIGHEST

def upwind(field, west_side, east_side, courant_u, courant_v):
    south_side = jnp.roll(field, 1, axis=-1)
    north_side = jnp.roll(field, -1, axis=-1)
    return field - jnp.maximum(courant_u, 0.0) * (field - west_side) - jnp.minimum(courant_u, 0.0) * (east_side - field) - jnp.maximum(courant_v, 0.0) * (field - south_side) - jnp.minimum(courant_v, 0.0) * (north_side - field)

def finish(gram, innov, anomaly, mean_state):
    total = gram.shape[0]
    eye = jnp.eye(total, dtype=jnp.float32)
    smat = eye + gram / (total - 1)
    scale = jnp.sqrt(jnp.sum(smat * smat))
    ymat = smat / scale
    zmat = eye
    for sweep_id in range(SWEEPS):
        middle = 1.5 * eye - 0.5 * jnp.dot(zmat, ymat, precision=highest)
        ymat = jnp.dot(ymat, middle, precision=highest)
        zmat = jnp.dot(middle, zmat, precision=highest)
    weights_a = zmat / jnp.sqrt(scale)
    inverse = jnp.dot(zmat, zmat, precision=highest) / scale
    weights_m = jnp.dot(inverse, innov, precision=highest) / (total - 1)
    gmat = weights_a + weights_m[:, None]
    return mean_state[None, :] + jnp.dot(gmat.T, anomaly, precision=highest)

def analyse(ensemble, index_row, bin_row, value_row, weight_row, count, table):
    mean_state = lax.optimization_barrier(jnp.mean(ensemble, axis=0))
    anomaly = ensemble - mean_state[None, :]
    observed = jnp.take(ensemble, index_row, axis=1)
    obs_mean = lax.optimization_barrier(jnp.mean(observed, axis=0))
    spread = observed - obs_mean[None, :]
    slots = jnp.arange(index_row.shape[0])
    live = (slots < count * BLOCK).astype(jnp.float32)
    weighted = live * weight_row * jnp.take(table, bin_row)
    gram = jnp.dot(spread * weighted[None, :], spread.T, precision=highest)
    innov = jnp.dot(spread, weighted * (value_row - obs_mean), precision=highest)
    return finish(gram, innov, anomaly, mean_state)

def reference(state, u_courant, v_courant, obs_index, obs_bin, obs_value, obs_weight, obs_blocks, loc_table):
    fields = state.reshape(K, F, L, NX, NY)

    def advance(member_field):
        for turn_index in range(2):
            zero_row = jnp.zeros_like(member_field[..., :1, :])
            west_side = jnp.concatenate([zero_row, member_field[..., :-1, :]], axis=-2)
            east_side = jnp.concatenate([member_field[..., 1:, :], zero_row], axis=-2)
            member_field = upwind(member_field, west_side, east_side, u_courant, v_courant)
        return member_field
    background = lax.map(advance, fields).reshape(K, C, NPATCH, PATCH)

    def one_patch(patch_id):
        ensemble = lax.dynamic_slice_in_dim(background, patch_id, 1, 2).reshape(K, C * PATCH)
        return analyse(ensemble, obs_index[patch_id], obs_bin[patch_id], obs_value[patch_id], obs_weight[patch_id], obs_blocks[patch_id], loc_table)
    results = lax.map(one_patch, jnp.arange(NPATCH, dtype=jnp.int32))
    results = results.reshape(NPATCH, K, C, PATCH).transpose(1, 2, 0, 3)
    return results.reshape(K, C, NX, NY)
```

```python
import functools

import jax
import jax.numpy as jnp
from jax import lax
from jax.experimental import pallas as pl
from jax.experimental.pallas import tpu as pltpu
from jax.sharding import PartitionSpec as P

BLOCK = 128
SWEEPS = 8
LEVELS = 4
MESH = pl.DeviceIdType.MESH
F32 = jnp.float32
highest = lax.Precision.HIGHEST


def mm(a, b, over):
    return lax.dot_general(
        a, b, (over, ((), ())), precision=highest, preferred_element_type=F32
    )


def inverse_root_weights(acc, total):
    row = lax.broadcasted_iota(jnp.int32, (total, total), 0)
    col = lax.broadcasted_iota(jnp.int32, (total, total), 1)
    eye = (row == col).astype(F32)
    smat = eye + acc[:, :total] * (1.0 / (total - 1))
    innov = acc[:, total : total + 1]
    scale = jnp.sqrt(jnp.sum(jnp.sum(smat * smat, axis=1, keepdims=True), axis=0, keepdims=True))
    ymat = smat / scale
    zmat = eye
    nn = ((1,), (0,))
    for sweep in range(SWEEPS):
        middle = 1.5 * eye - 0.5 * (ymat if sweep == 0 else mm(zmat, ymat, nn))
        if sweep < SWEEPS - 1:
            ymat = mm(ymat, middle, nn)
        zmat = middle if sweep == 0 else mm(middle, zmat, nn)
    inverse = mm(zmat, zmat, nn) / scale
    mean_weights = jnp.sum(inverse * innov, axis=0, keepdims=True) * (1.0 / (total - 1))
    return zmat.T / jnp.sqrt(scale) + mean_weights


def kernel(
    tiles,
    state, u, v, obs_index, obs_bin, obs_value, obs_weight, obs_blocks, loc_table,
    out,
    raw, bg, par, par_raw, halo, coef, uv_halo, parts, hilo, dens, mean,
    load_sem, mate_ss, mate_rs, raw_ss, raw_rs, face_ss, face_rs,
    fwd_ss, fwd_rs, ret_ss, ret_rs, out_sem,
):
    members, channels, rows, width = state.shape
    half = rows // 2
    groups = members // 8
    total = 2 * members
    slots = obs_index.shape[1]
    m, t = lax.axis_index("member"), lax.axis_index("tile")
    core = lax.rem(t, 2)
    sign = 1 - 2 * core
    first = core * (rows - 1)
    row_of = lambda e: first + sign * e
    is_edge = m == core
    partner = (1 - m, t)
    mate = (m, t + sign)
    facing = (1 - m, lax.rem(t - sign + tiles, tiles))
    rc = lambda src, dst, ss, rs, to: pltpu.make_async_remote_copy(
        src_ref=src, dst_ref=dst, send_sem=ss, recv_sem=rs, device_id=to, device_id_type=MESH
    )

    def load(e):
        @pl.loop(0, channels)
        def _(c):
            pltpu.make_async_copy(
                state.at[:, c, row_of(e), :], raw.at[e, c], load_sem.at[e]
            ).start()

    def loaded(e):
        pltpu.make_async_copy(raw.at[e], raw.at[e], load_sem.at[e]).wait()

    order = [0, 1, rows - 1, rows - 2] + list(range(2, rows - 2))
    for e in order:
        load(e)

    barrier = pltpu.get_barrier_semaphore()
    for peer in (partner, mate):
        pl.semaphore_signal(barrier, inc=1, device_id=peer, device_id_type=MESH)

    @pl.when(is_edge)
    def _():
        pl.semaphore_signal(barrier, inc=1, device_id=facing, device_id_type=MESH)
        pl.semaphore_wait(barrier, 3)

    @pl.when(jnp.logical_not(is_edge))
    def _():
        pl.semaphore_wait(barrier, 2)

    mate_copies = [
        rc(raw.at[rows - 1], raw.at[rows], mate_ss.at[0], mate_rs.at[0], mate),
        rc(raw.at[rows - 2], raw.at[rows + 1], mate_ss.at[1], mate_rs.at[1], mate),
        rc(u.at[:, row_of(rows - 1), :], uv_halo.at[0], mate_ss.at[2], mate_rs.at[2], mate),
        rc(v.at[:, row_of(rows - 1), :], uv_halo.at[1], mate_ss.at[3], mate_rs.at[3], mate),
    ]
    raw_copies = [
        rc(raw.at[e], par_raw.at[e], raw_ss.at[e], raw_rs.at[e], partner) for e in range(2)
    ]
    face_copies = [
        rc(raw.at[0], halo.at[1, 0], face_ss.at[0], face_rs.at[0], facing),
        rc(raw.at[1], halo.at[1, 1], face_ss.at[1], face_rs.at[1], facing),
        rc(u.at[:, row_of(0), :], uv_halo.at[2], face_ss.at[2], face_rs.at[2], facing),
        rc(v.at[:, row_of(0), :], uv_halo.at[3], face_ss.at[3], face_rs.at[3], facing),
    ]
    relay_copies = [
        rc(par_raw.at[e], halo.at[0, e], face_ss.at[4 + e], face_rs.at[4 + e], facing)
        for e in range(2)
    ]
    sent_from = jnp.where(is_edge, half, 0)
    forward = lambda i: rc(bg.at[sent_from + i], par.at[i], fwd_ss.at[i], fwd_rs.at[i], partner)

    loaded(0)
    loaded(1)

    @pl.when(jnp.logical_not(is_edge))
    def _():
        for copy in raw_copies:
            copy.start()

    loaded(rows - 1)
    loaded(rows - 2)
    for copy in mate_copies:
        copy.start()

    @pl.when(is_edge)
    def _():
        for copy in face_copies:
            copy.start()

    signf = sign.astype(F32)
    inner = t - sign
    at_rim = jnp.logical_or(inner < 0, inner >= tiles)
    keep = jnp.where(at_rim, 0.0, 1.0).astype(F32)

    def set_coef(e, level, cu, cv):
        cu = cu * signf
        up, um = jnp.maximum(cu, 0.0), jnp.maximum(-cu, 0.0)
        vp, vm = jnp.maximum(cv, 0.0), jnp.maximum(-cv, 0.0)
        terms = [1.0 - up - um - vp - vm, up, um, vp, vm]
        if e == 0:
            terms.append(up * keep)
        for k, term in enumerate(terms):
            coef[e + 1, level, k] = jnp.broadcast_to(term, (8, width))

    for e in range(rows):
        for level in range(LEVELS):
            here = pl.ds(row_of(e), 1)
            set_coef(e, level, u[level, here, :], v[level, here, :])

    def step(e, level, west, q, east):
        c = lambda k: coef[e + 1, level, k]
        value = c(0) * q + c(3) * pltpu.roll(q, 1, 1) + c(4) * pltpu.roll(q, width - 1, 1)
        value = value + c(2) * east
        if west is not None:
            value = value + c(1) * west
        return value

    def advance(e0, n):
        @pl.loop(0, channels * groups)
        def _(i):
            c, level = i // groups, lax.rem(i // groups, LEVELS)
            here = pl.ds(pl.multiple_of(lax.rem(i, groups) * 8, 8), 8)
            q = {e: raw[e, c, here, :] for e in range(max(0, e0 - 2), e0 + n + 2)}
            once = {
                e: step(e, level, q.get(e - 1), q[e], q[e + 1])
                for e in range(max(0, e0 - 1), e0 + n + 1)
            }
            for e in range(e0, e0 + n):
                bg[e, c, here, :] = step(e, level, once.get(e - 1), once[e], once[e + 1])

    for e in range(2, rows - 2):
        loaded(e)
    advance(2, half - 2)

    @pl.when(jnp.logical_not(is_edge))
    def _():
        for i in range(2, half):
            forward(i).start()

    advance(0, 2)

    @pl.when(jnp.logical_not(is_edge))
    def _():
        for i in range(2):
            forward(i).start()

    for copy in mate_copies:
        copy.wait_recv()
    for level in range(LEVELS):
        set_coef(rows, level, uv_halo[0, pl.ds(level, 1), :], uv_halo[1, pl.ds(level, 1), :])
    advance(half, half)

    @pl.when(is_edge)
    def _():
        for i in range(half):
            forward(i).start()

    bins = obs_bin[...]
    local = jnp.zeros((rows, slots), F32)
    for b in range(loc_table.shape[0]):
        local = jnp.where(bins == b, loc_table[b], local)
    row_id = lax.broadcasted_iota(jnp.int32, (rows, slots), 0)
    live = jnp.zeros((rows, slots), jnp.int32)
    for r in range(rows):
        live = jnp.where(row_id == r, obs_blocks[r] * BLOCK, live)
    slot_id = lax.broadcasted_iota(jnp.int32, (rows, slots), 1)
    weight = jnp.where(slot_id < live, obs_weight[...] * local, 0.0)
    for k, term in enumerate((weight, weight * obs_value[...])):
        for piece in range(3):
            head = term.astype(jnp.bfloat16).astype(F32)
            parts[3 * k + piece] = head
            term = term - head
    index = obs_index[...]
    hilo[0] = ((index >> 7) & 3) * 16 + (index >> 9)
    hilo[1] = index & 127
    own_from = jnp.where(is_edge, 0, half)
    chunk = 512

    @pl.loop(0, half)
    def _(k):
        r = pl.ds(row_of(own_from + k), 1)

        def add(j, acc):
            at = pl.ds(pl.multiple_of(j * chunk, chunk), chunk)
            high = lax.broadcasted_iota(jnp.int32, (64, chunk), 0) == hilo[0, r, at]
            low = lax.broadcasted_iota(jnp.int32, (128, chunk), 0) == hilo[1, r, at]
            left = jnp.concatenate(
                [jnp.where(high, parts[p, r, at], 0.0).astype(jnp.bfloat16) for p in range(6)], axis=0
            )
            right = jnp.where(low, 1.0, 0.0).astype(jnp.bfloat16)
            return acc + lax.dot_general(
                left, right, (((1,), (1,)), ((), ())), preferred_element_type=F32
            )

        acc = lax.fori_loop(0, slots // chunk, add, jnp.zeros((384, 128), F32))
        for p in range(2):
            whole = acc[192 * p : 192 * p + 64]
            whole = whole + acc[192 * p + 64 : 192 * p + 128]
            whole = whole + acc[192 * p + 128 : 192 * p + 192]
            dens[k, p] = jnp.concatenate([whole[16 * q : 16 * q + 16] for q in range(4)], axis=1)

    @pl.when(is_edge)
    def _():
        for e in range(2):
            raw_copies[e].wait_recv()
            relay_copies[e].start()

    def add_halo():
        for level in range(LEVELS):
            here = pl.ds(level, 1)
            set_coef(-1, level, uv_halo[2, here, :], uv_halo[3, here, :])
        for near, at_edge, rows01 in ((0, raw, bg), (1, par_raw, par)):

            @pl.loop(0, channels * groups)
            def _(i):
                c, level = i // groups, lax.rem(i // groups, LEVELS)
                here = pl.ds(pl.multiple_of(lax.rem(i, groups) * 8, 8), 8)
                h1, h2 = halo[near, 0, c, here, :], halo[near, 1, c, here, :]
                once = step(-1, level, h2, h1, at_edge[0, c, here, :])
                inflow = coef[1, level, 5]
                z = inflow * h1
                first_row = inflow * once + coef[1, level, 0] * z
                first_row = first_row + coef[1, level, 3] * pltpu.roll(z, 1, 1)
                first_row = first_row + coef[1, level, 4] * pltpu.roll(z, width - 1, 1)
                rows01[0, c, here, :] += first_row
                rows01[1, c, here, :] += coef[2, level, 1] * z

    @pl.loop(0, half)
    def _(k):
        i = jnp.where(is_edge, lax.rem(k + 2, half), k)
        e = own_from + i
        late = jnp.logical_and(is_edge, k >= half - 2)

        @pl.when(jnp.logical_not(late))
        def _():
            forward(i).wait_recv()

        @pl.when(jnp.logical_and(late, k == half - 2))
        def _():
            for copy in face_copies + relay_copies:
                copy.wait_recv()
            for j in range(2):
                forward(j).wait_recv()
            add_halo()

        def both(c):
            return jnp.concatenate([bg[e, c], par[i, c]], axis=0)

        def add(c, acc):
            x = both(c)
            middle = jnp.sum(x, axis=0, keepdims=True) * (1.0 / total)
            mean[pl.ds(c, 1), :] = middle
            x = x - middle
            density = dens[i, 0, pl.ds(c, 1), :]
            departure = dens[i, 1, pl.ds(c, 1), :] - density * middle
            right = jnp.concatenate([x * density, jnp.broadcast_to(departure, (8, width))], axis=0)
            return acc + mm(x, right, ((1,), (1,)))

        acc = lax.fori_loop(0, channels, add, jnp.zeros((total, total + 8), F32))
        weights = inverse_root_weights(acc, total)

        @pl.loop(0, channels)
        def _(c):
            middle = mean[pl.ds(c, 1), :]
            x = middle + mm(weights, both(c) - middle, ((1,), (0,)))
            bg[e, c] = x[:members]
            par[i, c] = x[members:]
            place = out.at[:, c, row_of(e), :]
            rc(par.at[i, c], place, ret_ss.at[i], ret_rs.at[i], partner).start()
            pltpu.make_async_copy(bg.at[e, c], place, out_sem.at[i]).start()

    for i in range(half):
        forward(i).wait_send()
        pltpu.make_async_copy(bg.at[own_from + i], bg.at[own_from + i], out_sem.at[i]).wait()
        back = rc(par.at[i], out.at[:, :, row_of(sent_from + i), :], ret_ss.at[i], ret_rs.at[i], partner)
        back.wait_send()
        back.wait_recv()
    for copy in mate_copies:
        copy.wait_send()

    @pl.when(is_edge)
    def _():
        for copy in face_copies + relay_copies:
            copy.wait_send()

    @pl.when(jnp.logical_not(is_edge))
    def _():
        for copy in raw_copies:
            copy.wait_send()


def body(tiles, state, u, v, obs_index, obs_bin, obs_value, obs_weight, obs_blocks, loc_table):
    members, channels, rows, width = state.shape
    slots = obs_index.shape[1]
    half = rows // 2
    line = (channels, members, width)
    vmem = lambda *shape: pltpu.VMEM(shape, F32)
    dma = lambda n: pltpu.SemaphoreType.DMA((n,))
    anywhere = pl.BlockSpec(memory_space=pl.ANY)
    in_vmem = pl.BlockSpec(memory_space=pltpu.VMEM)
    in_smem = pl.BlockSpec(memory_space=pltpu.SMEM)
    return pl.pallas_call(
        functools.partial(kernel, tiles),
        out_shape=jax.ShapeDtypeStruct(state.shape, F32),
        in_specs=[anywhere] + [in_vmem] * 6 + [in_smem] * 2,
        out_specs=anywhere,
        scratch_shapes=[
            vmem(rows + 2, *line),
            vmem(rows, *line),
            vmem(half, *line),
            vmem(2, *line),
            vmem(2, 2, *line),
            vmem(rows + 2, LEVELS, 6, 8, width),
            vmem(4, LEVELS, width),
            vmem(6, rows, slots),
            pltpu.VMEM((2, rows, slots), jnp.int32),
            vmem(half, 2, 16, width),
            vmem(16, width),
            dma(rows), dma(4), dma(4), dma(2), dma(2), dma(6), dma(6),
            dma(half), dma(half), dma(half), dma(half), dma(half),
        ],
        compiler_params=pltpu.CompilerParams(
            collective_id=0, has_side_effects=True, vmem_limit_bytes=56 * 1024 * 1024
        ),
        name="filter_cycle",
    )(state, u, v, obs_index, obs_bin, obs_value, obs_weight, obs_blocks, loc_table)


def solution(mesh):
    placed = (
        P("member", None, "tile", None),
        P(None, "tile", None),
        P(None, "tile", None),
        P("tile", None),
        P("tile", None),
        P("tile", None),
        P("tile", None),
        P("tile"),
        P(),
    )
    return jax.shard_map(
        functools.partial(body, mesh.shape["tile"]),
        mesh=mesh,
        in_specs=placed,
        out_specs=P("member", None, "tile", None),
        check_vma=False,
    )
```

```python
import functools

import jax
import jax.numpy as jnp
from jax import lax
from jax.experimental import pallas as pl
from jax.experimental.pallas import tpu as pltpu
from jax.sharding import PartitionSpec as P

BLOCK = 128
SWEEPS = 8
LEVELS = 4
MESH = pl.DeviceIdType.MESH
F32 = jnp.float32
highest = lax.Precision.HIGHEST


def mm(a, b, over):
    return lax.dot_general(
        a, b, (over, ((), ())), precision=highest, preferred_element_type=F32
    )


def inverse_root_weights(acc, total):
    row = lax.broadcasted_iota(jnp.int32, (total, total), 0)
    col = lax.broadcasted_iota(jnp.int32, (total, total), 1)
    eye = (row == col).astype(F32)
    smat = eye + acc[:, :total] * (1.0 / (total - 1))
    innov = acc[:, total : total + 1]
    scale = jnp.sqrt(jnp.sum(jnp.sum(smat * smat, axis=1, keepdims=True), axis=0, keepdims=True))
    ymat = smat / scale
    zmat = eye
    nn = ((1,), (0,))
    for sweep in range(SWEEPS):
        middle = 1.5 * eye - 0.5 * (ymat if sweep == 0 else mm(zmat, ymat, nn))
        if sweep < SWEEPS - 1:
            ymat = mm(ymat, middle, nn)
        zmat = middle if sweep == 0 else mm(middle, zmat, nn)
    inverse = mm(zmat, zmat, nn) / scale
    mean_weights = jnp.sum(inverse * innov, axis=0, keepdims=True) * (1.0 / (total - 1))
    return zmat.T / jnp.sqrt(scale) + mean_weights


def kernel(
    tiles,
    state, u_in, v_in, index_in, bin_in, value_in, weight_in, obs_blocks, loc_table,
    out,
    u, v, obs_index, obs_bin, obs_value, obs_weight,
    raw, bg, par, par_raw, halo, coef, uv_halo, parts, hilo, dens, mean,
    load_sem, in_sem, mate_ss, mate_rs, raw_ss, raw_rs, face_ss, face_rs,
    fwd_ss, fwd_rs, ret_ss, ret_rs, out_sem,
):
    members, channels, rows, width = state.shape
    half = rows // 2
    groups = members // 8
    total = 2 * members
    slots = index_in.shape[1]
    m, t = lax.axis_index("member"), lax.axis_index("tile")
    core = lax.rem(t, 2)
    sign = 1 - 2 * core
    first = core * (rows - 1)
    row_of = lambda e: first + sign * e
    is_edge = m == core
    partner = (1 - m, t)
    mate = (m, t + sign)
    facing = (1 - m, lax.rem(t - sign + tiles, tiles))
    rc = lambda src, dst, ss, rs, to: pltpu.make_async_remote_copy(
        src_ref=src, dst_ref=dst, send_sem=ss, recv_sem=rs, device_id=to, device_id_type=MESH
    )

    barrier = pltpu.get_barrier_semaphore()
    for peer in (partner, mate):
        pl.semaphore_signal(barrier, inc=1, device_id=peer, device_id_type=MESH)

    @pl.when(is_edge)
    def _():
        pl.semaphore_signal(barrier, inc=1, device_id=facing, device_id_type=MESH)

    def load(e):
        @pl.loop(0, channels)
        def _(c):
            pltpu.make_async_copy(
                state.at[:, c, row_of(e), :], raw.at[e, c], load_sem.at[e]
            ).start()

    def loaded(e):
        pltpu.make_async_copy(raw.at[e], raw.at[e], load_sem.at[e]).wait()

    plain = [
        pltpu.make_async_copy(src, dst, in_sem.at[k])
        for k, (src, dst) in enumerate((
            (u_in, u), (v_in, v), (index_in, obs_index), (bin_in, obs_bin),
            (value_in, obs_value), (weight_in, obs_weight),
        ))
    ]
    for e in (0, 1, rows - 1, rows - 2):
        load(e)
    for copy in plain[:2]:
        copy.start()
    for e in range(2, rows - 2):
        load(e)
    for copy in plain[2:]:
        copy.start()

    @pl.when(is_edge)
    def _():
        pl.semaphore_wait(barrier, 3)

    @pl.when(jnp.logical_not(is_edge))
    def _():
        pl.semaphore_wait(barrier, 2)

    mate_copies = [
        rc(raw.at[rows - 1], raw.at[rows], mate_ss.at[0], mate_rs.at[0], mate),
        rc(raw.at[rows - 2], raw.at[rows + 1], mate_ss.at[1], mate_rs.at[1], mate),
        rc(u_in.at[:, row_of(rows - 1), :], uv_halo.at[0], mate_ss.at[2], mate_rs.at[2], mate),
        rc(v_in.at[:, row_of(rows - 1), :], uv_halo.at[1], mate_ss.at[3], mate_rs.at[3], mate),
    ]
    raw_copies = [
        rc(raw.at[e], par_raw.at[e], raw_ss.at[e], raw_rs.at[e], partner) for e in range(2)
    ]
    face_copies = [
        rc(raw.at[0], halo.at[1, 0], face_ss.at[0], face_rs.at[0], facing),
        rc(raw.at[1], halo.at[1, 1], face_ss.at[1], face_rs.at[1], facing),
        rc(u_in.at[:, row_of(0), :], uv_halo.at[2], face_ss.at[2], face_rs.at[2], facing),
        rc(v_in.at[:, row_of(0), :], uv_halo.at[3], face_ss.at[3], face_rs.at[3], facing),
    ]
    relay_copies = [
        rc(par_raw.at[e], halo.at[0, e], face_ss.at[4 + e], face_rs.at[4 + e], facing)
        for e in range(2)
    ]
    sent_from = jnp.where(is_edge, half, 0)
    forward = lambda i: rc(bg.at[sent_from + i], par.at[i], fwd_ss.at[i], fwd_rs.at[i], partner)

    loaded(0)
    loaded(1)

    @pl.when(jnp.logical_not(is_edge))
    def _():
        for copy in raw_copies:
            copy.start()

    loaded(rows - 1)
    loaded(rows - 2)
    for copy in mate_copies:
        copy.start()

    @pl.when(is_edge)
    def _():
        for copy in face_copies:
            copy.start()

    signf = sign.astype(F32)
    inner = t - sign
    at_rim = jnp.logical_or(inner < 0, inner >= tiles)
    keep = jnp.where(at_rim, 0.0, 1.0).astype(F32)

    def set_coef(e, level, cu, cv):
        cu = cu * signf
        up, um = jnp.maximum(cu, 0.0), jnp.maximum(-cu, 0.0)
        vp, vm = jnp.maximum(cv, 0.0), jnp.maximum(-cv, 0.0)
        terms = [1.0 - up - um - vp - vm, up, um, vp, vm]
        if e == 0:
            terms.append(up * keep)
        for k, term in enumerate(terms):
            coef[e + 1, level, k] = jnp.broadcast_to(term, (8, width))

    for copy in plain[:2]:
        copy.wait()
    for e in range(rows):
        for level in range(LEVELS):
            here = pl.ds(row_of(e), 1)
            set_coef(e, level, u[level, here, :], v[level, here, :])

    def step(e, level, west, q, east):
        c = lambda k: coef[e + 1, level, k]
        value = c(0) * q + c(3) * pltpu.roll(q, 1, 1) + c(4) * pltpu.roll(q, width - 1, 1)
        value = value + c(2) * east
        if west is not None:
            value = value + c(1) * west
        return value

    def advance(e0, n):
        @pl.loop(0, channels * groups)
        def _(i):
            c, level = i // groups, lax.rem(i // groups, LEVELS)
            here = pl.ds(pl.multiple_of(lax.rem(i, groups) * 8, 8), 8)
            q = {e: raw[e, c, here, :] for e in range(max(0, e0 - 2), e0 + n + 2)}
            once = {
                e: step(e, level, q.get(e - 1), q[e], q[e + 1])
                for e in range(max(0, e0 - 1), e0 + n + 1)
            }
            for e in range(e0, e0 + n):
                bg[e, c, here, :] = step(e, level, once.get(e - 1), once[e], once[e + 1])

    for e in range(2, rows - 2):
        loaded(e)
    advance(2, half - 2)

    @pl.when(jnp.logical_not(is_edge))
    def _():
        for i in range(2, half):
            forward(i).start()

    advance(0, 2)

    @pl.when(jnp.logical_not(is_edge))
    def _():
        for i in range(2):
            forward(i).start()

    for copy in mate_copies:
        copy.wait_recv()
    for level in range(LEVELS):
        set_coef(rows, level, uv_halo[0, pl.ds(level, 1), :], uv_halo[1, pl.ds(level, 1), :])
    advance(half, half)

    @pl.when(is_edge)
    def _():
        for i in range(half):
            forward(i).start()

    for copy in plain[2:]:
        copy.wait()
    bins = obs_bin[...]
    local = jnp.zeros((rows, slots), F32)
    for b in range(loc_table.shape[0]):
        local = jnp.where(bins == b, loc_table[b], local)
    row_id = lax.broadcasted_iota(jnp.int32, (rows, slots), 0)
    live = jnp.zeros((rows, slots), jnp.int32)
    for r in range(rows):
        live = jnp.where(row_id == r, obs_blocks[r] * BLOCK, live)
    slot_id = lax.broadcasted_iota(jnp.int32, (rows, slots), 1)
    weight = jnp.where(slot_id < live, obs_weight[...] * local, 0.0)
    for k, term in enumerate((weight, weight * obs_value[...])):
        for piece in range(3):
            head = term.astype(jnp.bfloat16).astype(F32)
            parts[3 * k + piece] = head
            term = term - head
    index = obs_index[...]
    hilo[0] = ((index >> 7) & 3) * 16 + (index >> 9)
    hilo[1] = index & 127
    own_from = jnp.where(is_edge, 0, half)
    chunk = 512

    @pl.loop(0, half)
    def _(k):
        r = pl.ds(row_of(own_from + k), 1)

        def add(j, acc):
            at = pl.ds(pl.multiple_of(j * chunk, chunk), chunk)
            high = lax.broadcasted_iota(jnp.int32, (64, chunk), 0) == hilo[0, r, at]
            low = lax.broadcasted_iota(jnp.int32, (128, chunk), 0) == hilo[1, r, at]
            left = jnp.concatenate(
                [jnp.where(high, parts[p, r, at], 0.0).astype(jnp.bfloat16) for p in range(6)], axis=0
            )
            right = jnp.where(low, 1.0, 0.0).astype(jnp.bfloat16)
            return acc + lax.dot_general(
                left, right, (((1,), (1,)), ((), ())), preferred_element_type=F32
            )

        acc = lax.fori_loop(0, slots // chunk, add, jnp.zeros((384, 128), F32))
        for p in range(2):
            whole = acc[192 * p : 192 * p + 64]
            whole = whole + acc[192 * p + 64 : 192 * p + 128]
            whole = whole + acc[192 * p + 128 : 192 * p + 192]
            dens[k, p] = jnp.concatenate([whole[16 * q : 16 * q + 16] for q in range(4)], axis=1)

    @pl.when(is_edge)
    def _():
        for e in range(2):
            raw_copies[e].wait_recv()
            relay_copies[e].start()

    def add_halo():
        for level in range(LEVELS):
            here = pl.ds(level, 1)
            set_coef(-1, level, uv_halo[2, here, :], uv_halo[3, here, :])
        for near, at_edge, rows01 in ((0, raw, bg), (1, par_raw, par)):

            @pl.loop(0, channels * groups)
            def _(i):
                c, level = i // groups, lax.rem(i // groups, LEVELS)
                here = pl.ds(pl.multiple_of(lax.rem(i, groups) * 8, 8), 8)
                h1, h2 = halo[near, 0, c, here, :], halo[near, 1, c, here, :]
                once = step(-1, level, h2, h1, at_edge[0, c, here, :])
                inflow = coef[1, level, 5]
                z = inflow * h1
                first_row = inflow * once + coef[1, level, 0] * z
                first_row = first_row + coef[1, level, 3] * pltpu.roll(z, 1, 1)
                first_row = first_row + coef[1, level, 4] * pltpu.roll(z, width - 1, 1)
                rows01[0, c, here, :] += first_row
                rows01[1, c, here, :] += coef[2, level, 1] * z

    @pl.loop(0, half)
    def _(k):
        i = jnp.where(is_edge, lax.rem(k + 2, half), k)
        e = own_from + i
        late = jnp.logical_and(is_edge, k >= half - 2)

        @pl.when(jnp.logical_not(late))
        def _():
            forward(i).wait_recv()

        @pl.when(jnp.logical_and(late, k == half - 2))
        def _():
            for copy in face_copies + relay_copies:
                copy.wait_recv()
            for j in range(2):
                forward(j).wait_recv()
            add_halo()

        def both(c):
            return jnp.concatenate([bg[e, c], par[i, c]], axis=0)

        def add(c, acc):
            x = both(c)
            middle = jnp.sum(x, axis=0, keepdims=True) * (1.0 / total)
            mean[pl.ds(c, 1), :] = middle
            x = x - middle
            density = dens[i, 0, pl.ds(c, 1), :]
            departure = dens[i, 1, pl.ds(c, 1), :] - density * middle
            right = jnp.concatenate([x * density, jnp.broadcast_to(departure, (8, width))], axis=0)
            return acc + mm(x, right, ((1,), (1,)))

        acc = lax.fori_loop(0, channels, add, jnp.zeros((total, total + 8), F32))
        weights = inverse_root_weights(acc, total)

        @pl.loop(0, channels)
        def _(c):
            middle = mean[pl.ds(c, 1), :]
            x = middle + mm(weights, both(c) - middle, ((1,), (0,)))
            bg[e, c] = x[:members]
            par[i, c] = x[members:]
            place = out.at[:, c, row_of(e), :]
            rc(par.at[i, c], place, ret_ss.at[i], ret_rs.at[i], partner).start()
            pltpu.make_async_copy(bg.at[e, c], place, out_sem.at[i]).start()

    for i in range(half):
        forward(i).wait_send()
        pltpu.make_async_copy(bg.at[own_from + i], bg.at[own_from + i], out_sem.at[i]).wait()
        back = rc(par.at[i], out.at[:, :, row_of(sent_from + i), :], ret_ss.at[i], ret_rs.at[i], partner)
        back.wait_send()
        back.wait_recv()
    for copy in mate_copies:
        copy.wait_send()

    @pl.when(is_edge)
    def _():
        for copy in face_copies + relay_copies:
            copy.wait_send()

    @pl.when(jnp.logical_not(is_edge))
    def _():
        for copy in raw_copies:
            copy.wait_send()


def body(tiles, state, u, v, obs_index, obs_bin, obs_value, obs_weight, obs_blocks, loc_table):
    members, channels, rows, width = state.shape
    slots = obs_index.shape[1]
    half = rows // 2
    line = (channels, members, width)
    vmem = lambda *shape: pltpu.VMEM(shape, F32)
    dma = lambda n: pltpu.SemaphoreType.DMA((n,))
    anywhere = pl.BlockSpec(memory_space=pl.ANY)
    in_smem = pl.BlockSpec(memory_space=pltpu.SMEM)
    return pl.pallas_call(
        functools.partial(kernel, tiles),
        out_shape=pltpu.VMEM(state.shape, F32),
        in_specs=[anywhere] * 7 + [in_smem] * 2,
        out_specs=anywhere,
        scratch_shapes=[
            vmem(*u.shape),
            vmem(*v.shape),
            pltpu.VMEM(obs_index.shape, jnp.int32),
            pltpu.VMEM(obs_bin.shape, jnp.int32),
            vmem(*obs_value.shape),
            vmem(*obs_weight.shape),
            vmem(rows + 2, *line),
            vmem(rows, *line),
            vmem(half, *line),
            vmem(2, *line),
            vmem(2, 2, *line),
            vmem(rows + 2, LEVELS, 6, 8, width),
            vmem(4, LEVELS, width),
            vmem(6, rows, slots),
            pltpu.VMEM((2, rows, slots), jnp.int32),
            vmem(half, 2, 16, width),
            vmem(16, width),
            dma(rows), dma(6), dma(4), dma(4), dma(2), dma(2), dma(6), dma(6),
            dma(half), dma(half), dma(half), dma(half), dma(half),
        ],
        compiler_params=pltpu.CompilerParams(
            collective_id=0, has_side_effects=True, vmem_limit_bytes=56 * 1024 * 1024
        ),
        name="filter_cycle",
    )(state, u, v, obs_index, obs_bin, obs_value, obs_weight, obs_blocks, loc_table)


def solution(mesh):
    placed = (
        P("member", None, "tile", None),
        P(None, "tile", None),
        P(None, "tile", None),
        P("tile", None),
        P("tile", None),
        P("tile", None),
        P("tile", None),
        P("tile"),
        P(),
    )
    return jax.shard_map(
        functools.partial(body, mesh.shape["tile"]),
        mesh=mesh,
        in_specs=placed,
        out_specs=P("member", None, "tile", None),
        check_vma=False,
    )
```

```python
import functools

import jax
import jax.numpy as jnp
from jax import lax
from jax.experimental import pallas as pl
from jax.experimental.pallas import tpu as pltpu
from jax.sharding import PartitionSpec as P

BLOCK = 128
SWEEPS = 8
LEVELS = 4
MESH = pl.DeviceIdType.MESH
F32 = jnp.float32
highest = lax.Precision.HIGHEST


def mm(a, b, over):
    return lax.dot_general(
        a, b, (over, ((), ())), precision=highest, preferred_element_type=F32
    )


def inverse_root_weights(acc, total):
    row = lax.broadcasted_iota(jnp.int32, (total, total), 0)
    col = lax.broadcasted_iota(jnp.int32, (total, total), 1)
    eye = (row == col).astype(F32)
    smat = eye + acc[:, :total] * (1.0 / (total - 1))
    innov = acc[:, total : total + 1]
    scale = jnp.sqrt(jnp.sum(jnp.sum(smat * smat, axis=1, keepdims=True), axis=0, keepdims=True))
    ymat = smat / scale
    zmat = eye
    nn = ((1,), (0,))
    for sweep in range(SWEEPS):
        middle = 1.5 * eye - 0.5 * (ymat if sweep == 0 else mm(zmat, ymat, nn))
        if sweep < SWEEPS - 1:
            ymat = mm(ymat, middle, nn)
        zmat = middle if sweep == 0 else mm(middle, zmat, nn)
    inverse = mm(zmat, zmat, nn) / scale
    mean_weights = jnp.sum(inverse * innov, axis=0, keepdims=True) * (1.0 / (total - 1))
    return zmat.T / jnp.sqrt(scale) + mean_weights


def kernel(
    tiles,
    state, u_in, v_in, index_in, bin_in, value_in, weight_in, obs_blocks, loc_table,
    out,
    u, v, obs_index, obs_bin, obs_value, obs_weight,
    raw, bg, par, halo, bracket, once, coef, parts, slot_weight, hilo, dens, mean,
    seen, seen_par, wmat, wmat_send,
    load_sem, in_sem, mate_ss, mate_rs, face_ss, face_rs, fwd_ss, fwd_rs, ret_ss, ret_rs,
    seen_ss, seen_rs, w_ss, w_rs, bracket_ss, bracket_rs, out_sem, edge_sem,
):
    members, channels, rows, width = state.shape
    half = rows // 2
    groups = members // 8
    total = 2 * members
    slots = index_in.shape[1]
    m, t = lax.axis_index("member"), lax.axis_index("tile")
    core = lax.rem(t, 2)
    sign = 1 - 2 * core
    first = core * (rows - 1)
    row_of = lambda e: first + sign * e
    is_edge = m == core
    partner = (1 - m, t)
    mate = (m, t + sign)
    facing = (1 - m, lax.rem(t - sign + tiles, tiles))
    rc = lambda src, dst, ss, rs, to: pltpu.make_async_remote_copy(
        src_ref=src, dst_ref=dst, send_sem=ss, recv_sem=rs, device_id=to, device_id_type=MESH
    )

    barrier = pltpu.get_barrier_semaphore()
    for peer in (partner, mate, facing):
        pl.semaphore_signal(barrier, inc=1, device_id=peer, device_id_type=MESH)

    def load(e):
        @pl.loop(0, channels)
        def _(c):
            pltpu.make_async_copy(
                state.at[:, c, row_of(e), :], raw.at[e + 1, c], load_sem.at[e]
            ).start()

    def loaded(e):
        pltpu.make_async_copy(raw.at[e + 1], raw.at[e + 1], load_sem.at[e]).wait()

    plain = [
        pltpu.make_async_copy(src, dst, in_sem.at[k])
        for k, (src, dst) in enumerate((
            (u_in, u.at[:, pl.ds(0, rows), :]), (v_in, v.at[:, pl.ds(0, rows), :]), (index_in, obs_index), (bin_in, obs_bin),
            (value_in, obs_value), (weight_in, obs_weight),
        ))
    ]
    start = jnp.where(is_edge, half, 2)
    around = [start + d for d in (0, -1, 1, -2, 2)]
    others = [lax.rem(start + d, rows) for d in range(3, rows - 2)]
    for copy in plain[:2]:
        copy.start()
    for e in around + others:
        load(e)
    for copy in plain[2:]:
        copy.start()

    pl.semaphore_wait(barrier, 3)

    mate_copies = [
        rc(raw.at[rows], raw.at[rows + 1], mate_ss.at[0], mate_rs.at[0], mate),
        rc(raw.at[rows - 1], raw.at[rows + 2], mate_ss.at[1], mate_rs.at[1], mate),
        rc(u_in.at[:, row_of(rows - 1), :], u.at[:, rows, :], mate_ss.at[2], mate_rs.at[2], mate),
        rc(v_in.at[:, row_of(rows - 1), :], v.at[:, rows, :], mate_ss.at[3], mate_rs.at[3], mate),
    ]
    face_copies = [
        rc(raw.at[1], halo.at[0], face_ss.at[0], face_rs.at[0], facing),
        rc(raw.at[2], halo.at[1], face_ss.at[1], face_rs.at[1], facing),
        rc(u_in.at[:, row_of(0), :], u.at[:, rows + 1, :], face_ss.at[2], face_rs.at[2], facing),
        rc(v_in.at[:, row_of(0), :], v.at[:, rows + 1, :], face_ss.at[3], face_rs.at[3], facing),
    ]
    sent_from = jnp.where(is_edge, half, 0)
    seen_copy = lambda j: rc(seen.at[j], seen_par.at[j], seen_ss.at[j], seen_rs.at[j], partner)
    w_copy = lambda j: rc(wmat_send.at[j], wmat.at[j], w_ss.at[j], w_rs.at[j], partner)
    bracket_copy = lambda j, src, dst: rc(src, dst, bracket_ss.at[j], bracket_rs.at[j], partner)
    forward = lambda i: rc(bg.at[sent_from + i], par.at[i], fwd_ss.at[i], fwd_rs.at[i], partner)

    signf = sign.astype(F32)
    inner = t - sign
    at_rim = jnp.logical_or(inner < 0, inner >= tiles)
    keep = jnp.where(at_rim, 0.0, 1.0).astype(F32)

    def set_coef(e, level):
        r = jnp.where(e == rows, rows, jnp.where(e < 0, rows + 1, row_of(e)))
        cu, cv = u[level, pl.ds(r, 1), :] * signf, v[level, pl.ds(r, 1), :]
        up, um = jnp.maximum(cu, 0.0), jnp.maximum(-cu, 0.0)
        vp, vm = jnp.maximum(cv, 0.0), jnp.maximum(-cv, 0.0)
        inflow = up * jnp.where(e == 0, keep, 1.0)
        for k, term in enumerate((1.0 - up - um - vp - vm, inflow, um, vp, vm)):
            coef[e + 1, level, k] = jnp.broadcast_to(term, (8, width))

    lanes = 128
    parts_of_row = width // lanes
    lane = lax.broadcasted_iota(jnp.int32, (8, lanes), 1)

    def sweep_level(level, e, source, west, east, target):
        for p in range(parts_of_row):
            here, south, north = (
                pl.ds((p + d) % parts_of_row * lanes, lanes) for d in (0, parts_of_row - 1, 1)
            )
            term = [coef[e + 1, level, k, :, here] for k in range(5)]
            for c in range(channels // LEVELS):
                for g in range(groups):
                    at = lambda x: (c * LEVELS + level, pl.ds(g * 8, 8), x)
                    q = source[at(here)]
                    below = pltpu.roll(jnp.where(lane == lanes - 1, source[at(south)], q), 1, 1)
                    above = pltpu.roll(jnp.where(lane == 0, source[at(north)], q), lanes - 1, 1)
                    value = term[0] * q + term[3] * below + term[4] * above
                    if east is not None:
                        value = value + term[2] * east[at(here)]
                    if west is not None:
                        value = value + term[1] * west[at(here)]
                    target[at(here)] = value

    def sweep(*args):
        @pl.loop(0, LEVELS)
        def _(level):
            sweep_level(level, *args)

    def scale(e, k, source, target):
        @pl.loop(0, channels * groups)
        def _(i):
            c = i // groups
            here = pl.ds(pl.multiple_of(lax.rem(i, groups) * 8, 8), 8)
            target[c, here, :] = coef[e + 1, lax.rem(c, LEVELS), k] * source[c, here, :]

    step_one = lambda e: (e, raw.at[e + 1], raw.at[e], raw.at[e + 2], once.at[e + 1])
    step_two = lambda e: (e, once.at[e + 1], once.at[e], once.at[e + 2], bg.at[e])
    own_from = jnp.where(is_edge, 0, half)
    for copy in plain[:2]:
        copy.wait()
    for e in around:
        loaded(e)

    @pl.loop(0, LEVELS)
    def _(level):
        @pl.loop(start - 1, start + 2)
        def _(e):
            set_coef(e, level)
            sweep_level(level, *step_one(e))

        sweep_level(level, *step_two(start))
        i = start - sent_from
        for f in range(channels // LEVELS):
            c = f * LEVELS + level
            rc(bg.at[start, c], par.at[i, c], fwd_ss.at[i], fwd_rs.at[i], partner).start()

    for e in others:
        loaded(e)
    for copy in mate_copies + face_copies[2:] + face_copies[:2]:
        copy.start()
    raw[0] = jnp.zeros(raw.shape[1:], F32)

    ahead = rows - 1 - start

    @pl.loop(0, rows - 2)
    def _(k):
        up = k < ahead
        e = jnp.where(up, start + 1 + k, start - 1 - (k - ahead))
        new = jnp.where(up, e + 1, e - 1)

        @pl.when(new == rows - 1)
        def _():
            for copy in mate_copies:
                copy.wait_recv()

        @pl.loop(0, LEVELS)
        def _(level):
            set_coef(new, level)
            sweep_level(level, *step_one(new))
            sweep_level(level, *step_two(e))

        @pl.when(jnp.where(is_edge, e >= half, jnp.logical_and(e >= 2, e < half)))
        def _():
            forward(e - sent_from).start()

    for copy in face_copies[2:]:
        copy.wait_recv()

    @pl.loop(0, LEVELS)
    def _(level):
        set_coef(-1, level)

    scale(-1, 2, raw.at[1], once.at[0])
    sweep(*step_two(0))

    for copy in plain[2:]:
        copy.wait()
    bins = obs_bin[...]
    local = jnp.zeros((rows, slots), F32)
    for b in range(loc_table.shape[0]):
        local = jnp.where(bins == b, loc_table[b], local)
    row_id = lax.broadcasted_iota(jnp.int32, (rows, slots), 0)
    live = jnp.zeros((rows, slots), jnp.int32)
    for r in range(rows):
        live = jnp.where(row_id == r, obs_blocks[r] * BLOCK, live)
    slot_id = lax.broadcasted_iota(jnp.int32, (rows, slots), 1)
    weight = jnp.where(slot_id < live, obs_weight[...] * local, 0.0)
    for k, term in enumerate((weight, weight * obs_value[...])):
        slot_weight[k] = term
        for piece in range(3):
            head = term.astype(jnp.bfloat16).astype(F32)
            parts[3 * k + piece] = head
            term = term - head
    index = obs_index[...]
    hilo[0] = ((index >> 7) & 3) * 16 + (index >> 9)
    hilo[1] = index & 127
    hilo[2] = index
    chunk = 512

    @pl.loop(jnp.where(is_edge, 2, 0), half)
    def _(k):
        r = pl.ds(row_of(own_from + k), 1)

        def add(j, acc):
            at = pl.ds(pl.multiple_of(j * chunk, chunk), chunk)
            high = lax.broadcasted_iota(jnp.int32, (64, chunk), 0) == hilo[0, r, at]
            low = lax.broadcasted_iota(jnp.int32, (128, chunk), 0) == hilo[1, r, at]
            left = jnp.concatenate(
                [jnp.where(high, parts[p, r, at], 0.0).astype(jnp.bfloat16) for p in range(6)], axis=0
            )
            right = jnp.where(low, 1.0, 0.0).astype(jnp.bfloat16)
            return acc + lax.dot_general(
                left, right, (((1,), (1,)), ((), ())), preferred_element_type=F32
            )

        acc = lax.fori_loop(0, slots // chunk, add, jnp.zeros((384, 128), F32))
        for p in range(2):
            whole = acc[192 * p : 192 * p + 64]
            whole = whole + acc[192 * p + 64 : 192 * p + 128]
            whole = whole + acc[192 * p + 128 : 192 * p + 192]
            dens[k, p] = jnp.concatenate([whole[16 * q : 16 * q + 16] for q in range(4)], axis=1)

    def look():
        for copy in face_copies[:2]:
            copy.wait_recv()
        sweep(-1, halo.at[0], halo.at[1], None, once.at[0])
        scale(0, 1, halo.at[0], once.at[1])
        sweep(0, once.at[1], once.at[0], None, halo.at[0])
        scale(1, 1, once.at[1], halo.at[1])

        @pl.loop(0, 2)
        def _(j):
            seen[j] = jnp.zeros((total, slots), F32)

            @pl.loop(0, channels)
            def _(c):
                x = jnp.concatenate([bg[j, c], halo[j, c]], axis=0)
                pieces = []
                for _ in range(3):
                    pieces.append(x.astype(jnp.bfloat16))
                    x = x - pieces[-1].astype(F32)
                left = jnp.concatenate(pieces, axis=0)
                entry = lax.broadcasted_iota(jnp.int32, (width, chunk), 0) + c * width
                for n in range(slots // chunk):
                    at = pl.ds(n * chunk, chunk)
                    hit = entry == hilo[2, pl.ds(row_of(j), 1), at]
                    found = lax.dot_general(
                        left, jnp.where(hit, 1.0, 0.0).astype(jnp.bfloat16),
                        (((1,), (0,)), ((), ())), preferred_element_type=F32,
                    )
                    found = found[:total] + found[total : 2 * total] + found[2 * total :]
                    seen[j, :, at] += found

            @pl.when(jnp.logical_not(is_edge))
            def _():
                seen_copy(j).start()

    def add(x, density, departure, acc):
        middle = jnp.sum(x, axis=0, keepdims=True) * (1.0 / total)
        x = x - middle
        departure = departure - density * middle
        right = jnp.concatenate([x * density, jnp.broadcast_to(departure, (8, width))], axis=0)
        return middle, acc + mm(x, right, ((1,), (1,)))

    nothing = jnp.zeros((total, total + 8), F32)

    def spread(j):
        weights = wmat[j, :, :total]

        @pl.loop(0, channels)
        def _(c):
            x = mm(weights, jnp.concatenate([bg[j, c], halo[j, c]], axis=0), ((1,), (0,)))
            bg[j, c] = x[:members]
            halo[j, c] = x[members:]
            bracket_copy(j, halo.at[j, c], bracket.at[j, c]).start()

    def lead():
        @pl.loop(0, 2)
        def _(j):
            seen_copy(j).wait_recv()
            r = pl.ds(row_of(j), 1)

            def columns(n, acc):
                at = pl.ds(pl.multiple_of(n * width, width), width)
                x = jnp.concatenate(
                    [
                        seen[j, :members, at] + seen_par[j, members:, at],
                        seen[j, members:, at] + seen_par[j, :members, at],
                    ],
                    axis=0,
                )
                return add(x, slot_weight[0, r, at], slot_weight[1, r, at], acc)[1]

            weights = inverse_root_weights(lax.fori_loop(0, slots // width, columns, nothing), total)
            weights = weights + (1.0 - jnp.sum(weights, axis=1, keepdims=True)) * (1.0 / total)
            wmat[j, :, :total] = weights
            turned = jnp.concatenate([weights[members:], weights[:members]], axis=0)
            wmat_send[j, :, :total] = jnp.concatenate(
                [turned[:, members:], turned[:, :members]], axis=1
            )
            w_copy(j).start()
            spread(j)

    def follow():
        @pl.loop(0, 2)
        def _(j):
            w_copy(j).wait_recv()
            spread(j)

    @pl.loop(0, half)
    def _(k):
        i = jnp.where(is_edge, k + 2, k)
        e = own_from + i

        @pl.when(k == jnp.where(is_edge, 0, 1))
        def _():
            look()

        @pl.when(jnp.logical_and(is_edge, k == half - 2))
        def _():
            lead()

        @pl.when(jnp.logical_and(jnp.logical_not(is_edge), k == half - 1))
        def _():
            follow()

        @pl.when(jnp.logical_or(jnp.logical_not(is_edge), k < half - 2))
        def _():
            forward(i).wait_recv()

            def both(c):
                return jnp.concatenate([bg[e, c], par[i, c]], axis=0)

            def column(c, acc):
                here = pl.ds(c, 1)
                middle, acc = add(both(c), dens[i, 0, here, :], dens[i, 1, here, :], acc)
                mean[here, :] = middle
                return acc

            weights = inverse_root_weights(lax.fori_loop(0, channels, column, nothing), total)

            @pl.loop(0, channels)
            def _(c):
                middle = mean[pl.ds(c, 1), :]
                x = middle + mm(weights, both(c) - middle, ((1,), (0,)))
                bg[e, c] = x[:members]
                par[i, c] = x[members:]
                place = out.at[:, c, row_of(e), :]
                rc(par.at[i, c], place, ret_ss.at[i], ret_rs.at[i], partner).start()
                pltpu.make_async_copy(bg.at[e, c], place, out_sem.at[i]).start()

    for j in range(2):
        bracket_copy(j, halo.at[j], bracket.at[j]).wait_recv()

        @pl.loop(0, channels)
        def _(c):
            bg[j, c] += bracket[j, c]
            pltpu.make_async_copy(bg.at[j, c], out.at[:, c, row_of(j), :], edge_sem.at[j]).start()

    back = lambda i: rc(
        par.at[i], out.at[:, :, row_of(sent_from + i), :], ret_ss.at[i], ret_rs.at[i], partner
    )

    def direct(i):
        pltpu.make_async_copy(bg.at[own_from + i], bg.at[own_from + i], out_sem.at[i]).wait()
        back(i).wait_send()

    @pl.when(is_edge)
    def _():
        for i in range(2, half):
            direct(i)
        for i in range(half):
            back(i).wait_recv()
            forward(i).wait_send()
        for j in range(2):
            w_copy(j).wait_send()

    @pl.when(jnp.logical_not(is_edge))
    def _():
        for i in range(half):
            direct(i)
        for i in range(2, half):
            back(i).wait_recv()
            forward(i).wait_send()
        for j in range(2):
            seen_copy(j).wait_send()

    for j in range(2):
        bracket_copy(j, halo.at[j], bracket.at[j]).wait_send()
        pltpu.make_async_copy(bg.at[j], bg.at[j], edge_sem.at[j]).wait()
    for copy in mate_copies + face_copies:
        copy.wait_send()


def body(tiles, state, u, v, obs_index, obs_bin, obs_value, obs_weight, obs_blocks, loc_table):
    members, channels, rows, width = state.shape
    slots = obs_index.shape[1]
    half = rows // 2
    line = (channels, members, width)
    vmem = lambda *shape: pltpu.VMEM(shape, F32)
    dma = lambda n: pltpu.SemaphoreType.DMA((n,))
    anywhere = pl.BlockSpec(memory_space=pl.ANY)
    in_smem = pl.BlockSpec(memory_space=pltpu.SMEM)
    return pl.pallas_call(
        functools.partial(kernel, tiles),
        out_shape=pltpu.VMEM(state.shape, F32),
        in_specs=[anywhere] * 7 + [in_smem] * 2,
        out_specs=anywhere,
        scratch_shapes=[
            vmem(LEVELS, 2 * rows, width),
            vmem(LEVELS, 2 * rows, width),
            pltpu.VMEM(obs_index.shape, jnp.int32),
            pltpu.VMEM(obs_bin.shape, jnp.int32),
            vmem(*obs_value.shape),
            vmem(*obs_weight.shape),
            vmem(rows + 3, *line),
            vmem(rows, *line),
            vmem(half, *line),
            vmem(2, *line),
            vmem(2, *line),
            vmem(rows + 2, *line),
            vmem(rows + 2, LEVELS, 5, 8, width),
            vmem(6, rows, slots),
            vmem(2, rows, slots),
            pltpu.VMEM((3, rows, slots), jnp.int32),
            vmem(half, 2, 16, width),
            vmem(16, width),
            vmem(2, 2 * members, slots),
            vmem(2, 2 * members, slots),
            vmem(2, 2 * members, 128),
            vmem(2, 2 * members, 128),
            dma(rows), dma(6), dma(4), dma(4), dma(4), dma(4), dma(half), dma(half), dma(half), dma(half),
            dma(2), dma(2), dma(2), dma(2), dma(2), dma(2), dma(half), dma(2),
        ],
        compiler_params=pltpu.CompilerParams(
            collective_id=0, has_side_effects=True, vmem_limit_bytes=56 * 1024 * 1024
        ),
        name="filter_cycle",
    )(state, u, v, obs_index, obs_bin, obs_value, obs_weight, obs_blocks, loc_table)


def solution(mesh):
    placed = (
        P("member", None, "tile", None),
        P(None, "tile", None),
        P(None, "tile", None),
        P("tile", None),
        P("tile", None),
        P("tile", None),
        P("tile", None),
        P("tile"),
        P(),
    )
    return jax.shard_map(
        functools.partial(body, mesh.shape["tile"]),
        mesh=mesh,
        in_specs=placed,
        out_specs=P("member", None, "tile", None),
        check_vma=False,
    )
```

```python
import functools

import jax
import jax.numpy as jnp
from jax import lax
from jax.experimental import pallas as pl
from jax.experimental.pallas import tpu as pltpu
from jax.sharding import PartitionSpec as P

BLOCK = 128
SWEEPS = 8
LEVELS = 4
MESH = pl.DeviceIdType.MESH
F32 = jnp.float32
highest = lax.Precision.HIGHEST


def mm(a, b, over):
    return lax.dot_general(
        a, b, (over, ((), ())), precision=highest, preferred_element_type=F32
    )


def inverse_root_weights(acc, total):
    row = lax.broadcasted_iota(jnp.int32, (total, total), 0)
    col = lax.broadcasted_iota(jnp.int32, (total, total), 1)
    eye = (row == col).astype(F32)
    smat = eye + acc[:, :total] * (1.0 / (total - 1))
    innov = acc[:, total : total + 1]
    scale = jnp.sqrt(jnp.sum(jnp.sum(smat * smat, axis=1, keepdims=True), axis=0, keepdims=True))
    ymat = smat / scale
    zmat = eye
    nn = ((1,), (0,))
    for sweep in range(SWEEPS):
        middle = 1.5 * eye - 0.5 * (ymat if sweep == 0 else mm(zmat, ymat, nn))
        if sweep < SWEEPS - 1:
            ymat = mm(ymat, middle, nn)
        zmat = middle if sweep == 0 else mm(middle, zmat, nn)
    inverse = mm(zmat, zmat, nn) / scale
    mean_weights = jnp.sum(inverse * innov, axis=0, keepdims=True) * (1.0 / (total - 1))
    return zmat.T / jnp.sqrt(scale) + mean_weights


def kernel(
    tiles,
    state, u_in, v_in, index_in, bin_in, value_in, weight_in, blocks_in, table_in,
    out,
    u, v, obs_index, obs_bin, obs_value, obs_weight, obs_blocks, loc_table,
    raw, bg, par, halo, bracket, once, coef, parts, slot_weight, hilo, dens, mean,
    seen, seen_par, wmat, wmat_send,
    load_sem, level_sem, in_sem, mate_ss, mate_rs, face_ss, face_rs, fwd_ss, fwd_rs, ret_ss, ret_rs,
    seen_ss, seen_rs, w_ss, w_rs, bracket_ss, bracket_rs, out_sem, edge_sem,
):
    members, channels, rows, width = state.shape
    half = rows // 2
    groups = members // 8
    total = 2 * members
    slots = index_in.shape[1]
    m, t = lax.axis_index("member"), lax.axis_index("tile")
    core = lax.rem(t, 2)
    sign = 1 - 2 * core
    first = core * (rows - 1)
    row_of = lambda e: first + sign * e
    is_edge = m == core
    partner = (1 - m, t)
    mate = (m, t + sign)
    facing = (1 - m, lax.rem(t - sign + tiles, tiles))
    rc = lambda src, dst, ss, rs, to: pltpu.make_async_remote_copy(
        src_ref=src, dst_ref=dst, send_sem=ss, recv_sem=rs, device_id=to, device_id_type=MESH
    )

    barrier = pltpu.get_barrier_semaphore()
    for peer in (partner, mate, facing):
        pl.semaphore_signal(barrier, inc=1, device_id=peer, device_id_type=MESH)

    fetch = lambda e, c, sem: pltpu.make_async_copy(
        state.at[:, c, row_of(e), :], raw.at[e + 1, c], sem
    )

    def load(e):
        @pl.loop(0, channels)
        def _(c):
            fetch(e, c, load_sem.at[e]).start()

    def loaded(e):
        pltpu.make_async_copy(raw.at[e + 1], raw.at[e + 1], load_sem.at[e]).wait()

    plain = [
        pltpu.make_async_copy(src, dst, in_sem.at[k])
        for k, (src, dst) in enumerate((
            (u_in, u.at[:, pl.ds(0, rows), :]), (v_in, v.at[:, pl.ds(0, rows), :]), (index_in, obs_index), (bin_in, obs_bin),
            (value_in, obs_value), (weight_in, obs_weight),
            (blocks_in, obs_blocks), (table_in, loc_table),
        ))
    ]
    start = jnp.where(is_edge, half, 2)
    others = [lax.rem(start + d, rows) for d in range(3, rows - 2)]
    for copy in plain[:2]:
        copy.start()

    @pl.loop(0, LEVELS)
    def _(level):
        @pl.loop(start - 2, start + 3)
        def _(e):
            for f in range(channels // LEVELS):
                fetch(e, f * LEVELS + level, level_sem.at[level]).start()

    for e in others:
        load(e)
    for copy in plain[2:]:
        copy.start()

    pl.semaphore_wait(barrier, 3)

    mate_copies = [
        rc(raw.at[rows], raw.at[rows + 1], mate_ss.at[0], mate_rs.at[0], mate),
        rc(raw.at[rows - 1], raw.at[rows + 2], mate_ss.at[1], mate_rs.at[1], mate),
        rc(u_in.at[:, row_of(rows - 1), :], u.at[:, rows, :], mate_ss.at[2], mate_rs.at[2], mate),
        rc(v_in.at[:, row_of(rows - 1), :], v.at[:, rows, :], mate_ss.at[3], mate_rs.at[3], mate),
    ]
    face_copies = [
        rc(raw.at[1], halo.at[0], face_ss.at[0], face_rs.at[0], facing),
        rc(raw.at[2], halo.at[1], face_ss.at[1], face_rs.at[1], facing),
        rc(u_in.at[:, row_of(0), :], u.at[:, rows + 1, :], face_ss.at[2], face_rs.at[2], facing),
        rc(v_in.at[:, row_of(0), :], v.at[:, rows + 1, :], face_ss.at[3], face_rs.at[3], facing),
    ]
    sent_from = jnp.where(is_edge, half, 0)
    seen_copy = lambda j: rc(seen.at[j], seen_par.at[j], seen_ss.at[j], seen_rs.at[j], partner)
    w_copy = lambda j: rc(wmat_send.at[j], wmat.at[j], w_ss.at[j], w_rs.at[j], partner)
    bracket_copy = lambda j, src, dst: rc(src, dst, bracket_ss.at[j], bracket_rs.at[j], partner)
    forward = lambda i: rc(bg.at[sent_from + i], par.at[i], fwd_ss.at[i], fwd_rs.at[i], partner)

    signf = sign.astype(F32)
    inner = t - sign
    at_rim = jnp.logical_or(inner < 0, inner >= tiles)
    keep = jnp.where(at_rim, 0.0, 1.0).astype(F32)

    def set_coef(e, level):
        r = jnp.where(e == rows, rows, jnp.where(e < 0, rows + 1, row_of(e)))
        cu, cv = u[level, pl.ds(r, 1), :] * signf, v[level, pl.ds(r, 1), :]
        up, um = jnp.maximum(cu, 0.0), jnp.maximum(-cu, 0.0)
        vp, vm = jnp.maximum(cv, 0.0), jnp.maximum(-cv, 0.0)
        inflow = up * jnp.where(e == 0, keep, 1.0)
        for k, term in enumerate((1.0 - up - um - vp - vm, inflow, um, vp, vm)):
            coef[e + 1, level, k] = jnp.broadcast_to(term, (8, width))

    lanes = 128
    parts_of_row = width // lanes
    lane = lax.broadcasted_iota(jnp.int32, (8, lanes), 1)

    def sweep_level(level, e, source, west, east, target):
        for p in range(parts_of_row):
            here, south, north = (
                pl.ds((p + d) % parts_of_row * lanes, lanes) for d in (0, parts_of_row - 1, 1)
            )
            term = [coef[e + 1, level, k, :, here] for k in range(5)]
            for c in range(channels // LEVELS):
                for g in range(groups):
                    at = lambda x: (c * LEVELS + level, pl.ds(g * 8, 8), x)
                    q = source[at(here)]
                    below = pltpu.roll(jnp.where(lane == lanes - 1, source[at(south)], q), 1, 1)
                    above = pltpu.roll(jnp.where(lane == 0, source[at(north)], q), lanes - 1, 1)
                    value = term[0] * q + term[3] * below + term[4] * above
                    if east is not None:
                        value = value + term[2] * east[at(here)]
                    if west is not None:
                        value = value + term[1] * west[at(here)]
                    target[at(here)] = value

    def sweep(*args):
        @pl.loop(0, LEVELS)
        def _(level):
            sweep_level(level, *args)

    def scale(e, k, source, target):
        @pl.loop(0, channels * groups)
        def _(i):
            c = i // groups
            here = pl.ds(pl.multiple_of(lax.rem(i, groups) * 8, 8), 8)
            target[c, here, :] = coef[e + 1, lax.rem(c, LEVELS), k] * source[c, here, :]

    step_one = lambda e: (e, raw.at[e + 1], raw.at[e], raw.at[e + 2], once.at[e + 1])
    step_two = lambda e: (e, once.at[e + 1], once.at[e], once.at[e + 2], bg.at[e])
    own_from = jnp.where(is_edge, 0, half)
    for copy in plain[:2]:
        copy.wait()

    @pl.loop(0, LEVELS)
    def _(level):
        some = raw.at[pl.ds(start - 1, 5), pl.ds(0, channels // LEVELS)]
        pltpu.make_async_copy(some, some, level_sem.at[level]).wait()

        @pl.loop(start - 1, start + 2)
        def _(e):
            set_coef(e, level)
            sweep_level(level, *step_one(e))

        sweep_level(level, *step_two(start))
        i = start - sent_from
        for f in range(channels // LEVELS):
            c = f * LEVELS + level
            rc(bg.at[start, c], par.at[i, c], fwd_ss.at[i], fwd_rs.at[i], partner).start()

    for e in others:
        loaded(e)
    for copy in mate_copies + face_copies[2:] + face_copies[:2]:
        copy.start()
    raw[0] = jnp.zeros(raw.shape[1:], F32)

    ahead = rows - 1 - start

    @pl.loop(0, rows - 2)
    def _(k):
        up = k < ahead
        e = jnp.where(up, start + 1 + k, start - 1 - (k - ahead))
        new = jnp.where(up, e + 1, e - 1)

        @pl.when(new == rows - 1)
        def _():
            for copy in mate_copies:
                copy.wait_recv()

        @pl.loop(0, LEVELS)
        def _(level):
            set_coef(new, level)
            sweep_level(level, *step_one(new))
            sweep_level(level, *step_two(e))

        @pl.when(jnp.where(is_edge, e >= half, jnp.logical_and(e >= 2, e < half)))
        def _():
            forward(e - sent_from).start()

    for copy in face_copies[2:]:
        copy.wait_recv()

    @pl.loop(0, LEVELS)
    def _(level):
        set_coef(-1, level)

    scale(-1, 2, raw.at[1], once.at[0])
    sweep(*step_two(0))

    for copy in plain[2:]:
        copy.wait()
    bins = obs_bin[...]
    local = jnp.zeros((rows, slots), F32)
    for b in range(loc_table.shape[0]):
        local = jnp.where(bins == b, loc_table[b], local)
    row_id = lax.broadcasted_iota(jnp.int32, (rows, slots), 0)
    live = jnp.zeros((rows, slots), jnp.int32)
    for r in range(rows):
        live = jnp.where(row_id == r, obs_blocks[r] * BLOCK, live)
    slot_id = lax.broadcasted_iota(jnp.int32, (rows, slots), 1)
    weight = jnp.where(slot_id < live, obs_weight[...] * local, 0.0)
    for k, term in enumerate((weight, weight * obs_value[...])):
        slot_weight[k] = term
        for piece in range(3):
            head = term.astype(jnp.bfloat16).astype(F32)
            parts[3 * k + piece] = head
            term = term - head
    index = obs_index[...]
    hilo[0] = ((index >> 7) & 3) * 16 + (index >> 9)
    hilo[1] = index & 127
    hilo[2] = index
    chunk = 512

    @pl.loop(jnp.where(is_edge, 2, 0), half)
    def _(k):
        r = pl.ds(row_of(own_from + k), 1)

        def add(j, acc):
            at = pl.ds(pl.multiple_of(j * chunk, chunk), chunk)
            high = lax.broadcasted_iota(jnp.int32, (64, chunk), 0) == hilo[0, r, at]
            low = lax.broadcasted_iota(jnp.int32, (128, chunk), 0) == hilo[1, r, at]
            left = jnp.concatenate(
                [jnp.where(high, parts[p, r, at], 0.0).astype(jnp.bfloat16) for p in range(6)], axis=0
            )
            right = jnp.where(low, 1.0, 0.0).astype(jnp.bfloat16)
            return acc + lax.dot_general(
                left, right, (((1,), (1,)), ((), ())), preferred_element_type=F32
            )

        acc = lax.fori_loop(0, slots // chunk, add, jnp.zeros((384, 128), F32))
        for p in range(2):
            whole = acc[192 * p : 192 * p + 64]
            whole = whole + acc[192 * p + 64 : 192 * p + 128]
            whole = whole + acc[192 * p + 128 : 192 * p + 192]
            dens[k, p] = jnp.concatenate([whole[16 * q : 16 * q + 16] for q in range(4)], axis=1)

    mine = jnp.where(is_edge, 0, 1)
    theirs = 1 - mine

    def look():
        for copy in face_copies[:2]:
            copy.wait_recv()
        sweep(-1, halo.at[0], halo.at[1], None, once.at[0])
        scale(0, 1, halo.at[0], once.at[1])
        sweep(0, once.at[1], once.at[0], None, halo.at[0])
        scale(1, 1, once.at[1], halo.at[1])

        @pl.loop(0, 2)
        def _(n):
            j = jnp.where(n == 0, theirs, mine)
            seen[j] = jnp.zeros((total, slots), F32)

            @pl.loop(0, channels)
            def _(c):
                x = jnp.concatenate([bg[j, c], halo[j, c]], axis=0)
                pieces = []
                for _ in range(3):
                    pieces.append(x.astype(jnp.bfloat16))
                    x = x - pieces[-1].astype(F32)
                left = jnp.concatenate(pieces, axis=0)
                entry = lax.broadcasted_iota(jnp.int32, (width, chunk), 0) + c * width
                for part in range(slots // chunk):
                    at = pl.ds(part * chunk, chunk)
                    hit = entry == hilo[2, pl.ds(row_of(j), 1), at]
                    found = lax.dot_general(
                        left, jnp.where(hit, 1.0, 0.0).astype(jnp.bfloat16),
                        (((1,), (0,)), ((), ())), preferred_element_type=F32,
                    )
                    found = found[:total] + found[total : 2 * total] + found[2 * total :]
                    seen[j, :, at] += found

            @pl.when(n == 0)
            def _():
                seen_copy(j).start()

    def add(x, density, departure, acc):
        middle = jnp.sum(x, axis=0, keepdims=True) * (1.0 / total)
        x = x - middle
        departure = departure - density * middle
        right = jnp.concatenate([x * density, jnp.broadcast_to(departure, (8, width))], axis=0)
        return middle, acc + mm(x, right, ((1,), (1,)))

    nothing = jnp.zeros((total, total + 8), F32)

    def spread(j):
        weights = wmat[j, :, :total]

        @pl.loop(0, channels)
        def _(c):
            x = mm(weights, jnp.concatenate([bg[j, c], halo[j, c]], axis=0), ((1,), (0,)))
            bg[j, c] = x[:members]
            halo[j, c] = x[members:]
            bracket_copy(j, halo.at[j, c], bracket.at[j, c]).start()

    def lead(j):
        seen_copy(j).wait_recv()
        r = pl.ds(row_of(j), 1)

        def columns(n, acc):
            at = pl.ds(pl.multiple_of(n * width, width), width)
            x = jnp.concatenate(
                [
                    seen[j, :members, at] + seen_par[j, members:, at],
                    seen[j, members:, at] + seen_par[j, :members, at],
                ],
                axis=0,
            )
            return add(x, slot_weight[0, r, at], slot_weight[1, r, at], acc)[1]

        weights = inverse_root_weights(lax.fori_loop(0, slots // width, columns, nothing), total)
        weights = weights + (1.0 - jnp.sum(weights, axis=1, keepdims=True)) * (1.0 / total)
        wmat[j, :, :total] = weights
        turned = jnp.concatenate([weights[members:], weights[:members]], axis=0)
        wmat_send[j, :, :total] = jnp.concatenate(
            [turned[:, members:], turned[:, :members]], axis=1
        )
        w_copy(j).start()


    @pl.loop(0, half)
    def _(k):
        i = jnp.where(is_edge, k + 2, k)
        e = own_from + i

        @pl.when(k == jnp.where(is_edge, 0, 1))
        def _():
            look()

        @pl.when(k == half - 2)
        def _():
            lead(mine)

        @pl.when(k == half - 1)
        def _():
            w_copy(theirs).wait_recv()

        @pl.when(k >= half - 2)
        def _():
            spread(jnp.where(k == half - 2, mine, theirs))

        @pl.when(jnp.logical_or(jnp.logical_not(is_edge), k < half - 2))
        def _():
            forward(i).wait_recv()

            def both(c):
                return jnp.concatenate([bg[e, c], par[i, c]], axis=0)

            def column(c, acc):
                here = pl.ds(c, 1)
                middle, acc = add(both(c), dens[i, 0, here, :], dens[i, 1, here, :], acc)
                mean[here, :] = middle
                return acc

            weights = inverse_root_weights(lax.fori_loop(0, channels, column, nothing), total)

            @pl.loop(0, channels)
            def _(c):
                middle = mean[pl.ds(c, 1), :]
                x = middle + mm(weights, both(c) - middle, ((1,), (0,)))
                bg[e, c] = x[:members]
                par[i, c] = x[members:]
                place = out.at[:, c, row_of(e), :]
                rc(par.at[i, c], place, ret_ss.at[i], ret_rs.at[i], partner).start()
                pltpu.make_async_copy(bg.at[e, c], place, out_sem.at[i]).start()

    for j in range(2):
        bracket_copy(j, halo.at[j], bracket.at[j]).wait_recv()

        @pl.loop(0, channels)
        def _(c):
            bg[j, c] += bracket[j, c]
            pltpu.make_async_copy(bg.at[j, c], out.at[:, c, row_of(j), :], edge_sem.at[j]).start()

    back = lambda i: rc(
        par.at[i], out.at[:, :, row_of(sent_from + i), :], ret_ss.at[i], ret_rs.at[i], partner
    )

    def direct(i):
        pltpu.make_async_copy(bg.at[own_from + i], bg.at[own_from + i], out_sem.at[i]).wait()
        back(i).wait_send()

    @pl.when(is_edge)
    def _():
        for i in range(2, half):
            direct(i)
        for i in range(half):
            back(i).wait_recv()
            forward(i).wait_send()

    @pl.when(jnp.logical_not(is_edge))
    def _():
        for i in range(half):
            direct(i)
        for i in range(2, half):
            back(i).wait_recv()
            forward(i).wait_send()

    for j in range(2):
        bracket_copy(j, halo.at[j], bracket.at[j]).wait_send()
        pltpu.make_async_copy(bg.at[j], bg.at[j], edge_sem.at[j]).wait()
    seen_copy(theirs).wait_send()
    w_copy(mine).wait_send()
    for copy in mate_copies + face_copies:
        copy.wait_send()


def body(tiles, state, u, v, obs_index, obs_bin, obs_value, obs_weight, obs_blocks, loc_table):
    members, channels, rows, width = state.shape
    slots = obs_index.shape[1]
    half = rows // 2
    line = (channels, members, width)
    vmem = lambda *shape: pltpu.VMEM(shape, F32)
    dma = lambda n: pltpu.SemaphoreType.DMA((n,))
    anywhere = pl.BlockSpec(memory_space=pl.ANY)
    return pl.pallas_call(
        functools.partial(kernel, tiles),
        out_shape=pltpu.VMEM(state.shape, F32),
        in_specs=[anywhere] * 9,
        out_specs=anywhere,
        scratch_shapes=[
            vmem(LEVELS, 2 * rows, width),
            vmem(LEVELS, 2 * rows, width),
            pltpu.VMEM(obs_index.shape, jnp.int32),
            pltpu.VMEM(obs_bin.shape, jnp.int32),
            vmem(*obs_value.shape),
            vmem(*obs_weight.shape),
            pltpu.SMEM(obs_blocks.shape, jnp.int32),
            pltpu.SMEM(loc_table.shape, F32),
            vmem(rows + 3, *line),
            vmem(rows, *line),
            vmem(half, *line),
            vmem(2, *line),
            vmem(2, *line),
            vmem(rows + 2, *line),
            vmem(rows + 2, LEVELS, 5, 8, width),
            vmem(6, rows, slots),
            vmem(2, rows, slots),
            pltpu.VMEM((3, rows, slots), jnp.int32),
            vmem(half, 2, 16, width),
            vmem(16, width),
            vmem(2, 2 * members, slots),
            vmem(2, 2 * members, slots),
            vmem(2, 2 * members, 128),
            vmem(2, 2 * members, 128),
            dma(rows), dma(LEVELS), dma(8), dma(4), dma(4), dma(4), dma(4), dma(half), dma(half), dma(half), dma(half),
            dma(2), dma(2), dma(2), dma(2), dma(2), dma(2), dma(half), dma(2),
        ],
        compiler_params=pltpu.CompilerParams(
            collective_id=0, has_side_effects=True, vmem_limit_bytes=56 * 1024 * 1024
        ),
        name="filter_cycle",
    )(state, u, v, obs_index, obs_bin, obs_value, obs_weight, obs_blocks, loc_table)


def solution(mesh):
    placed = (
        P("member", None, "tile", None),
        P(None, "tile", None),
        P(None, "tile", None),
        P("tile", None),
        P("tile", None),
        P("tile", None),
        P("tile", None),
        P("tile"),
        P(),
    )
    return jax.shard_map(
        functools.partial(body, mesh.shape["tile"]),
        mesh=mesh,
        in_specs=placed,
        out_specs=P("member", None, "tile", None),
        check_vma=False,
    )
```

```python
import functools

import jax
import jax.numpy as jnp
from jax import lax
from jax.experimental import pallas as pl
from jax.experimental.pallas import tpu as pltpu
from jax.sharding import PartitionSpec as P

BLOCK = 128
SWEEPS = 8
LEVELS = 4
MESH = pl.DeviceIdType.MESH
F32 = jnp.float32
highest = lax.Precision.HIGHEST


def mm(a, b, over):
    return lax.dot_general(
        a, b, (over, ((), ())), precision=highest, preferred_element_type=F32
    )


def inverse_root_weights(acc, total):
    row = lax.broadcasted_iota(jnp.int32, (total, total), 0)
    col = lax.broadcasted_iota(jnp.int32, (total, total), 1)
    eye = (row == col).astype(F32)
    smat = eye + acc[:, :total] * (1.0 / (total - 1))
    innov = acc[:, total : total + 1]
    scale = jnp.sqrt(jnp.sum(jnp.sum(smat * smat, axis=1, keepdims=True), axis=0, keepdims=True))
    ymat = smat / scale
    zmat = eye
    nn = ((1,), (0,))
    for sweep in range(SWEEPS):
        middle = 1.5 * eye - 0.5 * (ymat if sweep == 0 else mm(zmat, ymat, nn))
        if sweep < SWEEPS - 1:
            ymat = mm(ymat, middle, nn)
        zmat = middle if sweep == 0 else mm(middle, zmat, nn)
    inverse = mm(zmat, zmat, nn) / scale
    mean_weights = jnp.sum(inverse * innov, axis=0, keepdims=True) * (1.0 / (total - 1))
    return zmat.T / jnp.sqrt(scale) + mean_weights


def kernel(
    tiles,
    state, u_in, v_in, index_in, bin_in, value_in, weight_in, blocks_in, table_in,
    out,
    u, v, obs_index, obs_bin, obs_value, obs_weight, obs_blocks, loc_table,
    raw, bg, par, halo, bracket, once, coef, parts, slot_weight, hilo, dens, mean,
    seen, seen_par, wmat, wmat_send,
    load_sem, level_sem, in_sem, mate_ss, mate_rs, face_ss, face_rs, fwd_ss, fwd_rs, ret_ss, ret_rs,
    seen_ss, seen_rs, w_ss, w_rs, bracket_ss, bracket_rs, out_sem, edge_sem,
):
    members, channels, rows, width = state.shape
    half = rows // 2
    groups = members // 8
    total = 2 * members
    slots = index_in.shape[1]
    m, t = lax.axis_index("member"), lax.axis_index("tile")
    core = lax.rem(t, 2)
    sign = 1 - 2 * core
    first = core * (rows - 1)
    row_of = lambda e: first + sign * e
    is_edge = m == core
    partner = (1 - m, t)
    mate = (m, t + sign)
    facing = (1 - m, lax.rem(t - sign + tiles, tiles))
    rc = lambda src, dst, ss, rs, to: pltpu.make_async_remote_copy(
        src_ref=src, dst_ref=dst, send_sem=ss, recv_sem=rs, device_id=to, device_id_type=MESH
    )

    barrier = pltpu.get_barrier_semaphore()
    for peer in (partner, mate, facing):
        pl.semaphore_signal(barrier, inc=1, device_id=peer, device_id_type=MESH)

    fetch = lambda e, c, sem: pltpu.make_async_copy(
        state.at[:, c, row_of(e), :], raw.at[e + 1, c], sem
    )

    def load(e):
        @pl.loop(0, channels)
        def _(c):
            fetch(e, c, load_sem.at[e]).start()

    def loaded(e):
        pltpu.make_async_copy(raw.at[e + 1], raw.at[e + 1], load_sem.at[e]).wait()

    plain = [
        pltpu.make_async_copy(src, dst, in_sem.at[k])
        for k, (src, dst) in enumerate((
            (u_in, u.at[:, pl.ds(0, rows), :]), (v_in, v.at[:, pl.ds(0, rows), :]), (index_in, obs_index), (bin_in, obs_bin),
            (value_in, obs_value), (weight_in, obs_weight),
            (blocks_in, obs_blocks), (table_in, loc_table),
        ))
    ]
    start = jnp.where(is_edge, half, 2)
    others = [lax.rem(start + d, rows) for d in range(3, rows - 2)]
    for copy in plain[:2]:
        copy.start()

    @pl.loop(0, LEVELS)
    def _(level):
        @pl.loop(start - 2, start + 3)
        def _(e):
            for f in range(channels // LEVELS):
                fetch(e, f * LEVELS + level, level_sem.at[level]).start()

    mate_copies = [
        rc(raw.at[rows], raw.at[rows + 1], mate_ss.at[0], mate_rs.at[0], mate),
        rc(raw.at[rows - 1], raw.at[rows + 2], mate_ss.at[1], mate_rs.at[1], mate),
        rc(u_in.at[:, row_of(rows - 1), :], u.at[:, rows, :], mate_ss.at[2], mate_rs.at[2], mate),
        rc(v_in.at[:, row_of(rows - 1), :], v.at[:, rows, :], mate_ss.at[3], mate_rs.at[3], mate),
    ]
    face_copies = [
        rc(raw.at[1], halo.at[0], face_ss.at[0], face_rs.at[0], facing),
        rc(raw.at[2], halo.at[1], face_ss.at[1], face_rs.at[1], facing),
        rc(u_in.at[:, row_of(0), :], u.at[:, rows + 1, :], face_ss.at[2], face_rs.at[2], facing),
        rc(v_in.at[:, row_of(0), :], v.at[:, rows + 1, :], face_ss.at[3], face_rs.at[3], facing),
    ]
    sent_from = jnp.where(is_edge, half, 0)
    seen_copy = lambda j: rc(seen.at[j], seen_par.at[j], seen_ss.at[j], seen_rs.at[j], partner)
    w_copy = lambda j: rc(wmat_send.at[j], wmat.at[j], w_ss.at[j], w_rs.at[j], partner)
    bracket_copy = lambda j, src, dst: rc(src, dst, bracket_ss.at[j], bracket_rs.at[j], partner)
    forward = lambda i: rc(bg.at[sent_from + i], par.at[i], fwd_ss.at[i], fwd_rs.at[i], partner)

    signf = sign.astype(F32)
    inner = t - sign
    at_rim = jnp.logical_or(inner < 0, inner >= tiles)
    keep = jnp.where(at_rim, 0.0, 1.0).astype(F32)

    def set_coef(e, level):
        r = jnp.where(e == rows, rows, jnp.where(e < 0, rows + 1, row_of(e)))
        cu, cv = u[level, pl.ds(r, 1), :] * signf, v[level, pl.ds(r, 1), :]
        up, um = jnp.maximum(cu, 0.0), jnp.maximum(-cu, 0.0)
        vp, vm = jnp.maximum(cv, 0.0), jnp.maximum(-cv, 0.0)
        inflow = up * jnp.where(e == 0, keep, 1.0)
        for k, term in enumerate((1.0 - up - um - vp - vm, inflow, um, vp, vm)):
            coef[e + 1, level, k] = jnp.broadcast_to(term, (8, width))

    lanes = 128
    parts_of_row = width // lanes
    lane = lax.broadcasted_iota(jnp.int32, (8, lanes), 1)

    def sweep_level(level, e, source, west, east, target):
        for p in range(parts_of_row):
            here, south, north = (
                pl.ds((p + d) % parts_of_row * lanes, lanes) for d in (0, parts_of_row - 1, 1)
            )
            term = [coef[e + 1, level, k, :, here] for k in range(5)]
            for c in range(channels // LEVELS):
                for g in range(groups):
                    at = lambda x: (c * LEVELS + level, pl.ds(g * 8, 8), x)
                    q = source[at(here)]
                    below = pltpu.roll(jnp.where(lane == lanes - 1, source[at(south)], q), 1, 1)
                    above = pltpu.roll(jnp.where(lane == 0, source[at(north)], q), lanes - 1, 1)
                    value = term[0] * q + term[3] * below + term[4] * above
                    if east is not None:
                        value = value + term[2] * east[at(here)]
                    if west is not None:
                        value = value + term[1] * west[at(here)]
                    target[at(here)] = value

    def sweep(*args):
        @pl.loop(0, LEVELS)
        def _(level):
            sweep_level(level, *args)

    def scale(e, k, source, target):
        @pl.loop(0, channels * groups)
        def _(i):
            c = i // groups
            here = pl.ds(pl.multiple_of(lax.rem(i, groups) * 8, 8), 8)
            target[c, here, :] = coef[e + 1, lax.rem(c, LEVELS), k] * source[c, here, :]

    step_one = lambda e: (e, raw.at[e + 1], raw.at[e], raw.at[e + 2], once.at[e + 1])
    step_two = lambda e: (e, once.at[e + 1], once.at[e], once.at[e + 2], bg.at[e])
    own_from = jnp.where(is_edge, 0, half)
    for copy in plain[:2]:
        copy.wait()

    @pl.loop(0, LEVELS)
    def _(level):
        some = raw.at[pl.ds(start - 1, 5), pl.ds(0, channels // LEVELS)]
        pltpu.make_async_copy(some, some, level_sem.at[level]).wait()

        @pl.loop(start - 1, start + 2)
        def _(e):
            set_coef(e, level)
            sweep_level(level, *step_one(e))

        sweep_level(level, *step_two(start))
        i = start - sent_from

        @pl.when(level == 0)
        def _():
            pl.semaphore_wait(barrier, 3)

        for f in range(channels // LEVELS):
            c = f * LEVELS + level
            rc(bg.at[start, c], par.at[i, c], fwd_ss.at[i], fwd_rs.at[i], partner).start()

        @pl.when(level == 0)
        def _():
            for e in others:
                load(e)
            for copy in plain[2:]:
                copy.start()

    for e in others:
        loaded(e)
    for copy in mate_copies + face_copies[2:] + face_copies[:2]:
        copy.start()
    raw[0] = jnp.zeros(raw.shape[1:], F32)

    ahead = rows - 1 - start

    @pl.loop(0, rows - 2)
    def _(k):
        up = k < ahead
        e = jnp.where(up, start + 1 + k, start - 1 - (k - ahead))
        new = jnp.where(up, e + 1, e - 1)

        @pl.when(new == rows - 1)
        def _():
            for copy in mate_copies:
                copy.wait_recv()

        @pl.loop(0, LEVELS)
        def _(level):
            set_coef(new, level)
            sweep_level(level, *step_one(new))
            sweep_level(level, *step_two(e))

        @pl.when(jnp.where(is_edge, e >= half, jnp.logical_and(e >= 2, e < half)))
        def _():
            forward(e - sent_from).start()

    for copy in face_copies[2:]:
        copy.wait_recv()

    @pl.loop(0, LEVELS)
    def _(level):
        set_coef(-1, level)

    scale(-1, 2, raw.at[1], once.at[0])
    sweep(*step_two(0))

    for copy in plain[2:]:
        copy.wait()
    bins = obs_bin[...]
    local = jnp.zeros((rows, slots), F32)
    for b in range(loc_table.shape[0]):
        local = jnp.where(bins == b, loc_table[b], local)
    row_id = lax.broadcasted_iota(jnp.int32, (rows, slots), 0)
    live = jnp.zeros((rows, slots), jnp.int32)
    for r in range(rows):
        live = jnp.where(row_id == r, obs_blocks[r] * BLOCK, live)
    slot_id = lax.broadcasted_iota(jnp.int32, (rows, slots), 1)
    weight = jnp.where(slot_id < live, obs_weight[...] * local, 0.0)
    for k, term in enumerate((weight, weight * obs_value[...])):
        slot_weight[k] = term
        for piece in range(3):
            head = term.astype(jnp.bfloat16).astype(F32)
            parts[3 * k + piece] = head
            term = term - head
    index = obs_index[...]
    hilo[0] = ((index >> 7) & 3) * 16 + (index >> 9)
    hilo[1] = index & 127
    hilo[2] = index
    chunk = 512

    @pl.loop(jnp.where(is_edge, 2, 0), half)
    def _(k):
        r = pl.ds(row_of(own_from + k), 1)

        def add(j, acc):
            at = pl.ds(pl.multiple_of(j * chunk, chunk), chunk)
            high = lax.broadcasted_iota(jnp.int32, (64, chunk), 0) == hilo[0, r, at]
            low = lax.broadcasted_iota(jnp.int32, (128, chunk), 0) == hilo[1, r, at]
            left = jnp.concatenate(
                [jnp.where(high, parts[p, r, at], 0.0).astype(jnp.bfloat16) for p in range(6)], axis=0
            )
            right = jnp.where(low, 1.0, 0.0).astype(jnp.bfloat16)
            return acc + lax.dot_general(
                left, right, (((1,), (1,)), ((), ())), preferred_element_type=F32
            )

        acc = lax.fori_loop(0, slots // chunk, add, jnp.zeros((384, 128), F32))
        for p in range(2):
            whole = acc[192 * p : 192 * p + 64]
            whole = whole + acc[192 * p + 64 : 192 * p + 128]
            whole = whole + acc[192 * p + 128 : 192 * p + 192]
            dens[k, p] = jnp.concatenate([whole[16 * q : 16 * q + 16] for q in range(4)], axis=1)

    mine = jnp.where(is_edge, 0, 1)
    theirs = 1 - mine

    def look():
        for copy in face_copies[:2]:
            copy.wait_recv()
        sweep(-1, halo.at[0], halo.at[1], None, once.at[0])
        scale(0, 1, halo.at[0], once.at[1])
        sweep(0, once.at[1], once.at[0], None, halo.at[0])
        scale(1, 1, once.at[1], halo.at[1])

        @pl.loop(0, 2)
        def _(n):
            j = jnp.where(n == 0, theirs, mine)
            seen[j] = jnp.zeros((total, slots), F32)

            @pl.loop(0, channels)
            def _(c):
                x = jnp.concatenate([bg[j, c], halo[j, c]], axis=0)
                pieces = []
                for _ in range(3):
                    pieces.append(x.astype(jnp.bfloat16))
                    x = x - pieces[-1].astype(F32)
                left = jnp.concatenate(pieces, axis=0)
                entry = lax.broadcasted_iota(jnp.int32, (width, chunk), 0) + c * width
                for part in range(slots // chunk):
                    at = pl.ds(part * chunk, chunk)
                    hit = entry == hilo[2, pl.ds(row_of(j), 1), at]
                    found = lax.dot_general(
                        left, jnp.where(hit, 1.0, 0.0).astype(jnp.bfloat16),
                        (((1,), (0,)), ((), ())), preferred_element_type=F32,
                    )
                    found = found[:total] + found[total : 2 * total] + found[2 * total :]
                    seen[j, :, at] += found

            @pl.when(n == 0)
            def _():
                seen_copy(j).start()

    def add(x, density, departure, acc):
        middle = jnp.sum(x, axis=0, keepdims=True) * (1.0 / total)
        x = x - middle
        departure = departure - density * middle
        right = jnp.concatenate([x * density, jnp.broadcast_to(departure, (8, width))], axis=0)
        return middle, acc + mm(x, right, ((1,), (1,)))

    nothing = jnp.zeros((total, total + 8), F32)

    def spread(j):
        weights = wmat[j, :, :total]

        @pl.loop(0, channels)
        def _(c):
            x = mm(weights, jnp.concatenate([bg[j, c], halo[j, c]], axis=0), ((1,), (0,)))
            bg[j, c] = x[:members]
            halo[j, c] = x[members:]
            bracket_copy(j, halo.at[j, c], bracket.at[j, c]).start()

    def lead(j):
        seen_copy(j).wait_recv()
        r = pl.ds(row_of(j), 1)

        def columns(n, acc):
            at = pl.ds(pl.multiple_of(n * width, width), width)
            x = jnp.concatenate(
                [
                    seen[j, :members, at] + seen_par[j, members:, at],
                    seen[j, members:, at] + seen_par[j, :members, at],
                ],
                axis=0,
            )
            return add(x, slot_weight[0, r, at], slot_weight[1, r, at], acc)[1]

        weights = inverse_root_weights(lax.fori_loop(0, slots // width, columns, nothing), total)
        weights = weights + (1.0 - jnp.sum(weights, axis=1, keepdims=True)) * (1.0 / total)
        wmat[j, :, :total] = weights
        turned = jnp.concatenate([weights[members:], weights[:members]], axis=0)
        wmat_send[j, :, :total] = jnp.concatenate(
            [turned[:, members:], turned[:, :members]], axis=1
        )
        w_copy(j).start()


    @pl.loop(0, half)
    def _(k):
        i = jnp.where(is_edge, 2 + k // (half - 1), k)
        e = own_from + i

        @pl.when(k == jnp.where(is_edge, 0, 1))
        def _():
            look()

        @pl.when(k == half - 2)
        def _():
            lead(mine)

        @pl.when(k == half - 1)
        def _():
            w_copy(theirs).wait_recv()

        @pl.when(k >= half - 2)
        def _():
            spread(jnp.where(k == half - 2, mine, theirs))

        @pl.when(jnp.logical_or(jnp.logical_not(is_edge), lax.rem(k, half - 1) == 0))
        def _():
            forward(i).wait_recv()

            def both(c):
                return jnp.concatenate([bg[e, c], par[i, c]], axis=0)

            def column(c, acc):
                here = pl.ds(c, 1)
                middle, acc = add(both(c), dens[i, 0, here, :], dens[i, 1, here, :], acc)
                mean[here, :] = middle
                return acc

            weights = inverse_root_weights(lax.fori_loop(0, channels, column, nothing), total)

            @pl.loop(0, channels)
            def _(c):
                middle = mean[pl.ds(c, 1), :]
                x = middle + mm(weights, both(c) - middle, ((1,), (0,)))
                bg[e, c] = x[:members]
                par[i, c] = x[members:]
                place = out.at[:, c, row_of(e), :]
                rc(par.at[i, c], place, ret_ss.at[i], ret_rs.at[i], partner).start()
                pltpu.make_async_copy(bg.at[e, c], place, out_sem.at[i]).start()

    for j in range(2):
        bracket_copy(j, halo.at[j], bracket.at[j]).wait_recv()

        @pl.loop(0, channels)
        def _(c):
            bg[j, c] += bracket[j, c]
            pltpu.make_async_copy(bg.at[j, c], out.at[:, c, row_of(j), :], edge_sem.at[j]).start()

    back = lambda i: rc(
        par.at[i], out.at[:, :, row_of(sent_from + i), :], ret_ss.at[i], ret_rs.at[i], partner
    )

    def direct(i):
        pltpu.make_async_copy(bg.at[own_from + i], bg.at[own_from + i], out_sem.at[i]).wait()
        back(i).wait_send()

    @pl.when(is_edge)
    def _():
        for i in range(2, half):
            direct(i)
        for i in range(half):
            back(i).wait_recv()
            forward(i).wait_send()

    @pl.when(jnp.logical_not(is_edge))
    def _():
        for i in range(half):
            direct(i)
        for i in range(2, half):
            back(i).wait_recv()
            forward(i).wait_send()

    for j in range(2):
        bracket_copy(j, halo.at[j], bracket.at[j]).wait_send()
        pltpu.make_async_copy(bg.at[j], bg.at[j], edge_sem.at[j]).wait()
    seen_copy(theirs).wait_send()
    w_copy(mine).wait_send()
    for copy in mate_copies + face_copies:
        copy.wait_send()


def body(tiles, state, u, v, obs_index, obs_bin, obs_value, obs_weight, obs_blocks, loc_table):
    members, channels, rows, width = state.shape
    slots = obs_index.shape[1]
    half = rows // 2
    line = (channels, members, width)
    vmem = lambda *shape: pltpu.VMEM(shape, F32)
    dma = lambda n: pltpu.SemaphoreType.DMA((n,))
    anywhere = pl.BlockSpec(memory_space=pl.ANY)
    return pl.pallas_call(
        functools.partial(kernel, tiles),
        out_shape=pltpu.VMEM(state.shape, F32),
        in_specs=[anywhere] * 9,
        out_specs=anywhere,
        scratch_shapes=[
            vmem(LEVELS, 2 * rows, width),
            vmem(LEVELS, 2 * rows, width),
            pltpu.VMEM(obs_index.shape, jnp.int32),
            pltpu.VMEM(obs_bin.shape, jnp.int32),
            vmem(*obs_value.shape),
            vmem(*obs_weight.shape),
            pltpu.SMEM(obs_blocks.shape, jnp.int32),
            pltpu.SMEM(loc_table.shape, F32),
            vmem(rows + 3, *line),
            vmem(rows, *line),
            vmem(half, *line),
            vmem(2, *line),
            vmem(2, *line),
            vmem(rows + 2, *line),
            vmem(rows + 2, LEVELS, 5, 8, width),
            vmem(6, rows, slots),
            vmem(2, rows, slots),
            pltpu.VMEM((3, rows, slots), jnp.int32),
            vmem(half, 2, 16, width),
            vmem(16, width),
            vmem(2, 2 * members, slots),
            vmem(2, 2 * members, slots),
            vmem(2, 2 * members, 128),
            vmem(2, 2 * members, 128),
            dma(rows), dma(LEVELS), dma(8), dma(4), dma(4), dma(4), dma(4), dma(half), dma(half), dma(half), dma(half),
            dma(2), dma(2), dma(2), dma(2), dma(2), dma(2), dma(half), dma(2),
        ],
        compiler_params=pltpu.CompilerParams(
            collective_id=0, has_side_effects=True, vmem_limit_bytes=56 * 1024 * 1024
        ),
        name="filter_cycle",
    )(state, u, v, obs_index, obs_bin, obs_value, obs_weight, obs_blocks, loc_table)


def solution(mesh):
    placed = (
        P("member", None, "tile", None),
        P(None, "tile", None),
        P(None, "tile", None),
        P("tile", None),
        P("tile", None),
        P("tile", None),
        P("tile", None),
        P("tile"),
        P(),
    )
    return jax.shard_map(
        functools.partial(body, mesh.shape["tile"]),
        mesh=mesh,
        in_specs=placed,
        out_specs=P("member", None, "tile", None),
        check_vma=False,
    )
```

```python
import functools

import jax
import jax.numpy as jnp
from jax import lax
from jax.experimental import pallas as pl
from jax.experimental.pallas import tpu as pltpu
from jax.sharding import PartitionSpec as P

BLOCK = 128
SWEEPS = 8
LEVELS = 4
MESH = pl.DeviceIdType.MESH
F32 = jnp.float32
highest = lax.Precision.HIGHEST


def mm(a, b, over):
    return lax.dot_general(
        a, b, (over, ((), ())), precision=highest, preferred_element_type=F32
    )


def inverse_root_weights(acc, total):
    row = lax.broadcasted_iota(jnp.int32, (total, total), 0)
    col = lax.broadcasted_iota(jnp.int32, (total, total), 1)
    eye = (row == col).astype(F32)
    smat = eye + acc[:, :total] * (1.0 / (total - 1))
    innov = acc[:, total : total + 1]
    scale = jnp.sqrt(jnp.sum(jnp.sum(smat * smat, axis=1, keepdims=True), axis=0, keepdims=True))
    ymat = smat / scale
    zmat = eye
    nn = ((1,), (0,))
    for sweep in range(SWEEPS):
        middle = 1.5 * eye - 0.5 * (ymat if sweep == 0 else mm(zmat, ymat, nn))
        if sweep < SWEEPS - 1:
            ymat = mm(ymat, middle, nn)
        zmat = middle if sweep == 0 else mm(middle, zmat, nn)
    inverse = mm(zmat, zmat, nn) / scale
    mean_weights = jnp.sum(inverse * innov, axis=0, keepdims=True) * (1.0 / (total - 1))
    return zmat.T / jnp.sqrt(scale) + mean_weights


def kernel(
    tiles,
    state, u_in, v_in, index_in, bin_in, value_in, weight_in, blocks_in, table_in,
    out,
    u, v, obs_index, obs_bin, obs_value, obs_weight, obs_blocks, loc_table,
    raw, bg, par, halo, bracket, once, coef, parts, slot_weight, hilo, dens, mean, place_of, dens_seen, near, far, chosen,
    seen, seen_par, wmat, wmat_send,
    load_sem, level_sem, in_sem, mate_ss, mate_rs, face_ss, face_rs, fwd_ss, fwd_rs, ret_ss, ret_rs,
    seen_ss, seen_rs, w_ss, w_rs, bracket_ss, bracket_rs, out_sem, edge_sem,
):
    members, channels, rows, width = state.shape
    half = rows // 2
    groups = members // 8
    total = 2 * members
    slots = index_in.shape[1]
    m, t = lax.axis_index("member"), lax.axis_index("tile")
    core = lax.rem(t, 2)
    sign = 1 - 2 * core
    first = core * (rows - 1)
    row_of = lambda e: first + sign * e
    is_edge = m == core
    partner = (1 - m, t)
    mate = (m, t + sign)
    facing = (1 - m, lax.rem(t - sign + tiles, tiles))
    rc = lambda src, dst, ss, rs, to: pltpu.make_async_remote_copy(
        src_ref=src, dst_ref=dst, send_sem=ss, recv_sem=rs, device_id=to, device_id_type=MESH
    )

    barrier = pltpu.get_barrier_semaphore()
    for peer in (partner, mate, facing):
        pl.semaphore_signal(barrier, inc=1, device_id=peer, device_id_type=MESH)

    fetch = lambda e, c, sem: pltpu.make_async_copy(
        state.at[:, c, row_of(e), :], raw.at[e + 1, c], sem
    )

    def load(e):
        @pl.loop(0, channels)
        def _(c):
            fetch(e, c, load_sem.at[e]).start()

    def loaded(e):
        pltpu.make_async_copy(raw.at[e + 1], raw.at[e + 1], load_sem.at[e]).wait()

    plain = [
        pltpu.make_async_copy(src, dst, in_sem.at[k])
        for k, (src, dst) in enumerate((
            (u_in, u.at[:, pl.ds(0, rows), :]), (v_in, v.at[:, pl.ds(0, rows), :]), (index_in, obs_index), (bin_in, obs_bin),
            (value_in, obs_value), (weight_in, obs_weight),
            (blocks_in, obs_blocks), (table_in, loc_table),
        ))
    ]
    start = jnp.where(is_edge, half, 2)
    others = [lax.rem(start + d, rows) for d in range(3, rows - 2)]
    for copy in plain[:2]:
        copy.start()

    @pl.loop(0, LEVELS)
    def _(level):
        @pl.loop(start - 2, start + 3)
        def _(e):
            for f in range(channels // LEVELS):
                fetch(e, f * LEVELS + level, level_sem.at[level]).start()

    mate_copies = [
        rc(raw.at[rows], raw.at[rows + 1], mate_ss.at[0], mate_rs.at[0], mate),
        rc(raw.at[rows - 1], raw.at[rows + 2], mate_ss.at[1], mate_rs.at[1], mate),
        rc(u_in.at[:, row_of(rows - 1), :], u.at[:, rows, :], mate_ss.at[2], mate_rs.at[2], mate),
        rc(v_in.at[:, row_of(rows - 1), :], v.at[:, rows, :], mate_ss.at[3], mate_rs.at[3], mate),
    ]
    face_copies = [
        rc(raw.at[1], halo.at[0], face_ss.at[0], face_rs.at[0], facing),
        rc(raw.at[2], halo.at[1], face_ss.at[1], face_rs.at[1], facing),
        rc(u_in.at[:, row_of(0), :], u.at[:, rows + 1, :], face_ss.at[2], face_rs.at[2], facing),
        rc(v_in.at[:, row_of(0), :], v.at[:, rows + 1, :], face_ss.at[3], face_rs.at[3], facing),
    ]
    sent_from = jnp.where(is_edge, half, 0)
    seen_copy = lambda j: rc(seen.at[j], seen_par.at[j], seen_ss.at[j], seen_rs.at[j], partner)
    w_copy = lambda j: rc(wmat_send.at[j], wmat.at[j], w_ss.at[j], w_rs.at[j], partner)
    bracket_copy = lambda src, dst: rc(src, dst, bracket_ss.at[0], bracket_rs.at[0], partner)
    far_copy = rc(chosen, far, bracket_ss.at[1], bracket_rs.at[1], partner)
    forward = lambda i: rc(bg.at[sent_from + i], par.at[i], fwd_ss.at[i], fwd_rs.at[i], partner)

    signf = sign.astype(F32)
    inner = t - sign
    at_rim = jnp.logical_or(inner < 0, inner >= tiles)
    keep = jnp.where(at_rim, 0.0, 1.0).astype(F32)

    def set_coef(e, level):
        r = jnp.where(e == rows, rows, jnp.where(e < 0, rows + 1, row_of(e)))
        cu, cv = u[level, pl.ds(r, 1), :] * signf, v[level, pl.ds(r, 1), :]
        up, um = jnp.maximum(cu, 0.0), jnp.maximum(-cu, 0.0)
        vp, vm = jnp.maximum(cv, 0.0), jnp.maximum(-cv, 0.0)
        inflow = up * jnp.where(e == 0, keep, 1.0)
        for k, term in enumerate((1.0 - up - um - vp - vm, inflow, um, vp, vm)):
            coef[e + 1, level, k] = jnp.broadcast_to(term, (8, width))

    lanes = 128
    parts_of_row = width // lanes
    lane = lax.broadcasted_iota(jnp.int32, (8, lanes), 1)

    def sweep_level(level, e, source, west, east, target):
        for p in range(parts_of_row):
            here, south, north = (
                pl.ds((p + d) % parts_of_row * lanes, lanes) for d in (0, parts_of_row - 1, 1)
            )
            term = [coef[e + 1, level, k, :, here] for k in range(5)]
            for c in range(channels // LEVELS):
                for g in range(groups):
                    at = lambda x: (c * LEVELS + level, pl.ds(g * 8, 8), x)
                    q = source[at(here)]
                    below = pltpu.roll(jnp.where(lane == lanes - 1, source[at(south)], q), 1, 1)
                    above = pltpu.roll(jnp.where(lane == 0, source[at(north)], q), lanes - 1, 1)
                    value = term[0] * q + term[3] * below + term[4] * above
                    if east is not None:
                        value = value + term[2] * east[at(here)]
                    if west is not None:
                        value = value + term[1] * west[at(here)]
                    target[at(here)] = value

    def sweep(*args):
        @pl.loop(0, LEVELS)
        def _(level):
            sweep_level(level, *args)

    def scale(e, k, source, target):
        @pl.loop(0, channels * groups)
        def _(i):
            c = i // groups
            here = pl.ds(pl.multiple_of(lax.rem(i, groups) * 8, 8), 8)
            target[c, here, :] = coef[e + 1, lax.rem(c, LEVELS), k] * source[c, here, :]

    step_one = lambda e: (e, raw.at[e + 1], raw.at[e], raw.at[e + 2], once.at[e + 1])
    step_two = lambda e: (e, once.at[e + 1], once.at[e], once.at[e + 2], bg.at[e])
    own_from = jnp.where(is_edge, 0, half)
    for copy in plain[:2]:
        copy.wait()

    @pl.loop(0, LEVELS)
    def _(level):
        some = raw.at[pl.ds(start - 1, 5), pl.ds(0, channels // LEVELS)]
        pltpu.make_async_copy(some, some, level_sem.at[level]).wait()

        @pl.loop(start - 1, start + 2)
        def _(e):
            set_coef(e, level)
            sweep_level(level, *step_one(e))

        sweep_level(level, *step_two(start))
        i = start - sent_from

        @pl.when(level == 0)
        def _():
            pl.semaphore_wait(barrier, 3)

        for f in range(channels // LEVELS):
            c = f * LEVELS + level
            rc(bg.at[start, c], par.at[i, c], fwd_ss.at[i], fwd_rs.at[i], partner).start()

        @pl.when(level == 0)
        def _():
            for e in others:
                load(e)
            for copy in plain[2:]:
                copy.start()

    for e in others:
        loaded(e)
    for copy in mate_copies + face_copies[2:] + face_copies[:2]:
        copy.start()
    raw[0] = jnp.zeros(raw.shape[1:], F32)

    ahead = rows - 1 - start

    @pl.loop(0, rows - 2)
    def _(k):
        up = k < ahead
        e = jnp.where(up, start + 1 + k, start - 1 - (k - ahead))
        new = jnp.where(up, e + 1, e - 1)

        @pl.when(new == rows - 1)
        def _():
            for copy in mate_copies:
                copy.wait_recv()

        @pl.loop(0, LEVELS)
        def _(level):
            set_coef(new, level)
            sweep_level(level, *step_one(new))
            sweep_level(level, *step_two(e))

        @pl.when(jnp.where(is_edge, e >= half, jnp.logical_and(e >= 2, e < half)))
        def _():
            forward(e - sent_from).start()

    for copy in face_copies[2:]:
        copy.wait_recv()

    @pl.loop(0, LEVELS)
    def _(level):
        set_coef(-1, level)

    scale(-1, 2, raw.at[1], once.at[0])
    sweep(*step_two(0))

    for copy in plain[2:]:
        copy.wait()
    bins = obs_bin[...]
    local = jnp.zeros((rows, slots), F32)
    for b in range(loc_table.shape[0]):
        local = jnp.where(bins == b, loc_table[b], local)
    row_id = lax.broadcasted_iota(jnp.int32, (rows, slots), 0)
    live = jnp.zeros((rows, slots), jnp.int32)
    for r in range(rows):
        live = jnp.where(row_id == r, obs_blocks[r] * BLOCK, live)
    slot_id = lax.broadcasted_iota(jnp.int32, (rows, slots), 1)
    weight = jnp.where(slot_id < live, obs_weight[...] * local, 0.0)
    for k, term in enumerate((weight, weight * obs_value[...])):
        slot_weight[k] = term
        for piece in range(3):
            head = term.astype(jnp.bfloat16).astype(F32)
            parts[3 * k + piece] = head
            term = term - head
    index = obs_index[...]
    hilo[0] = ((index >> 7) & 3) * 16 + (index >> 9)
    hilo[1] = index & 127
    hilo[2] = index
    chunk = 512

    by_channel = lambda x: jnp.concatenate([x[16 * q : 16 * q + 16] for q in range(4)], axis=1)

    @pl.loop(jnp.where(is_edge, 2, 0), half + 2)
    def _(k):
        r = pl.ds(row_of(jnp.where(k < half, own_from + k, k - half)), 1)

        def add(j, acc):
            at = pl.ds(pl.multiple_of(j * chunk, chunk), chunk)
            high = lax.broadcasted_iota(jnp.int32, (64, chunk), 0) == hilo[0, r, at]
            low = lax.broadcasted_iota(jnp.int32, (128, chunk), 0) == hilo[1, r, at]
            left = jnp.concatenate(
                [jnp.where(high, parts[p, r, at], 0.0).astype(jnp.bfloat16) for p in range(6)]
                + [jnp.where(high, 1.0, 0.0).astype(jnp.bfloat16)],
                axis=0,
            )
            right = jnp.where(low, 1.0, 0.0).astype(jnp.bfloat16)
            return acc + lax.dot_general(
                left, right, (((1,), (1,)), ((), ())), preferred_element_type=F32
            )

        acc = lax.fori_loop(0, slots // chunk, add, jnp.zeros((448, 128), F32))
        for p in range(2):
            whole = acc[192 * p : 192 * p + 64]
            whole = whole + acc[192 * p + 64 : 192 * p + 128]
            whole = whole + acc[192 * p + 128 : 192 * p + 192]
            dens[k, p] = by_channel(whole)

        @pl.when(k >= half)
        def _():
            hit = jnp.where(acc[384:] > 0.0, 1.0, 0.0)
            iota = lambda shape, d: lax.broadcasted_iota(jnp.int32, shape, d)
            order = lambda x: (x & 15) * 4 + (x >> 4)
            square, lines = (128, 128), (64, 64)
            left_of = jnp.where(iota(square, 0) < iota(square, 1), 1.0, 0.0).astype(jnp.bfloat16)
            above = jnp.where(order(iota(lines, 1)) < order(iota(lines, 0)), 1.0, 0.0)
            count = jnp.broadcast_to(jnp.sum(hit, axis=1, keepdims=True), hit.shape)
            exact = lambda x, y: lax.dot_general(
                x.astype(jnp.bfloat16), y.astype(jnp.bfloat16),
                (((1,), (0,)), ((), ())), preferred_element_type=F32,
            )
            rank = exact(hit, left_of) + exact(above, count)
            entry = (order(iota(hit.shape, 0)) * 128 + iota(hit.shape, 1)).astype(F32)
            seen_count = jnp.sum(count[:, :1], axis=0, keepdims=True)
            place_of[k - half] = by_channel(
                jnp.where(hit > 0.0, rank, seen_count + entry - rank)
            )

    mine = jnp.where(is_edge, 0, 1)
    theirs = 1 - mine

    def pieces_of(x):
        pieces = []
        for _ in range(3):
            pieces.append(x.astype(jnp.bfloat16))
            x = x - pieces[-1].astype(F32)
        return jnp.concatenate(pieces, axis=0)

    def thirds(x):
        n = x.shape[0] // 3
        return x[:n] + x[n : 2 * n] + x[2 * n :]

    def hot(j, c, part):
        n = (lax.broadcasted_iota(jnp.int32, (chunk, width), 0) + part * chunk).astype(F32)
        return jnp.where(n == place_of[j, pl.ds(c, 1), :], 1.0, 0.0).astype(jnp.bfloat16)

    def pick(left, right, over):
        return thirds(
            lax.dot_general(left, right, (over, ((), ())), preferred_element_type=F32)
        )

    def look():
        for copy in face_copies[:2]:
            copy.wait_recv()
        sweep(-1, halo.at[0], halo.at[1], None, once.at[0])
        scale(0, 1, halo.at[0], once.at[1])
        sweep(0, once.at[1], once.at[0], None, halo.at[0])
        scale(1, 1, once.at[1], halo.at[1])

        @pl.loop(0, 2)
        def _(n):
            j = jnp.where(n == 0, theirs, mine)
            seen[j] = jnp.zeros((total, slots), F32)
            dens_seen[j] = jnp.zeros((8, slots), F32)

            @pl.loop(0, channels)
            def _(c):
                here = pl.ds(c, 1)
                blank = jnp.zeros((6, width), F32)
                left = pieces_of(
                    jnp.concatenate(
                        [bg[j, c], halo[j, c], dens[half + j, 0, here, :], dens[half + j, 1, here, :], blank],
                        axis=0,
                    )
                )
                for part in range(slots // chunk):
                    at = pl.ds(part * chunk, chunk)
                    found = pick(left, hot(j, c, part), ((1,), (1,)))
                    seen[j, :, at] += found[:total]
                    dens_seen[j, :, at] += found[total:]

            @pl.when(n == 0)
            def _():
                seen_copy(j).start()

    def add(x, density, departure, acc):
        middle = jnp.sum(x, axis=0, keepdims=True) * (1.0 / total)
        x = x - middle
        departure = departure - density * middle
        right = jnp.concatenate([x * density, jnp.broadcast_to(departure, (8, width))], axis=0)
        return middle, acc + mm(x, right, ((1,), (1,)))

    nothing = jnp.zeros((total, total + 8), F32)

    def spread(j):
        weights = wmat[j, :, :total]

        @pl.loop(0, channels)
        def _(c):
            x = mm(weights, jnp.concatenate([bg[j, c], halo[j, c]], axis=0), ((1,), (0,)))
            bg[j, c] = x[:members]
            halo[j, c] = x[members:]

            @pl.when(j == mine)
            def _():
                bracket_copy(halo.at[j, c], bracket.at[c]).start()

    def lead(j):
        seen_copy(j).wait_recv()

        def columns(n, acc):
            at = pl.ds(pl.multiple_of(n * width, width), width)
            x = jnp.concatenate(
                [
                    seen[j, :members, at] + seen_par[j, members:, at],
                    seen[j, members:, at] + seen_par[j, :members, at],
                ],
                axis=0,
            )
            return add(x, dens_seen[j, 0:1, at], dens_seen[j, 1:2, at], acc)[1]

        weights = inverse_root_weights(lax.fori_loop(0, slots // width, columns, nothing), total)
        weights = weights + (1.0 - jnp.sum(weights, axis=1, keepdims=True)) * (1.0 / total)
        wmat[j, :, :total] = weights
        turned = jnp.concatenate([weights[members:], weights[:members]], axis=0)
        wmat_send[j, :, :total] = jnp.concatenate(
            [turned[:, members:], turned[:, :members]], axis=1
        )
        w_copy(j).start()
        for part in range(slots // chunk):
            at = pl.ds(part * chunk, chunk)
            x = jnp.concatenate([seen_par[j, members:, at], seen_par[j, :members, at]], axis=0)
            near[:, at] = mm(weights[:members], x, ((1,), (0,)))

    def choose(j):
        chosen[...] = jnp.zeros(chosen.shape, F32)

        @pl.loop(0, channels)
        def _(c):
            left = pieces_of(halo[j, c])
            for part in range(chosen.shape[1] // chunk):
                at = pl.ds(part * chunk, chunk)
                chosen[:, at] += pick(left, hot(j, c, part + slots // chunk), ((1,), (1,)))

        far_copy.start()

    def gather_back(j, c, source, first):
        share = jnp.zeros((members, width), F32)
        for part in range(source.shape[1] // chunk):
            left = pieces_of(source[:, pl.ds(part * chunk, chunk)])
            share = share + pick(left, hot(j, c, first + part), ((1,), (0,)))
        return share

    @pl.loop(0, half)
    def _(k):
        i = jnp.where(is_edge, 2 + k // (half - 1), k)
        e = own_from + i

        @pl.when(k == jnp.where(is_edge, 0, 1))
        def _():
            look()

        @pl.when(k == half - 2)
        def _():
            lead(mine)

        @pl.when(k == half - 1)
        def _():
            w_copy(theirs).wait_recv()

        @pl.when(k >= half - 2)
        def _():
            spread(jnp.where(k == half - 2, mine, theirs))

        @pl.when(k == half - 1)
        def _():
            choose(theirs)

        @pl.when(jnp.logical_or(jnp.logical_not(is_edge), lax.rem(k, half - 1) == 0))
        def _():
            forward(i).wait_recv()

            def both(c):
                return jnp.concatenate([bg[e, c], par[i, c]], axis=0)

            def column(c, acc):
                here = pl.ds(c, 1)
                middle, acc = add(both(c), dens[i, 0, here, :], dens[i, 1, here, :], acc)
                mean[here, :] = middle
                return acc

            weights = inverse_root_weights(lax.fori_loop(0, channels, column, nothing), total)

            @pl.loop(0, channels)
            def _(c):
                middle = mean[pl.ds(c, 1), :]
                x = middle + mm(weights, both(c) - middle, ((1,), (0,)))
                bg[e, c] = x[:members]
                par[i, c] = x[members:]
                place = out.at[:, c, row_of(e), :]
                rc(par.at[i, c], place, ret_ss.at[i], ret_rs.at[i], partner).start()
                pltpu.make_async_copy(bg.at[e, c], place, out_sem.at[i]).start()

    def finish(j, share):
        @pl.loop(0, channels)
        def _(c):
            bg[j, c] += share(c)
            pltpu.make_async_copy(bg.at[j, c], out.at[:, c, row_of(j), :], edge_sem.at[j]).start()

    @pl.loop(0, channels)
    def _(c):
        bg[mine, c] += gather_back(mine, c, near, 0)

    bracket_copy(halo.at[mine], bracket).wait_recv()
    finish(theirs, lambda c: bracket[c])
    far_copy.wait_recv()
    finish(mine, lambda c: gather_back(mine, c, far, slots // chunk))

    back = lambda i: rc(
        par.at[i], out.at[:, :, row_of(sent_from + i), :], ret_ss.at[i], ret_rs.at[i], partner
    )

    def direct(i):
        pltpu.make_async_copy(bg.at[own_from + i], bg.at[own_from + i], out_sem.at[i]).wait()
        back(i).wait_send()

    @pl.when(is_edge)
    def _():
        for i in range(2, half):
            direct(i)
        for i in range(half):
            back(i).wait_recv()
            forward(i).wait_send()

    @pl.when(jnp.logical_not(is_edge))
    def _():
        for i in range(half):
            direct(i)
        for i in range(2, half):
            back(i).wait_recv()
            forward(i).wait_send()

    for j in range(2):
        pltpu.make_async_copy(bg.at[j], bg.at[j], edge_sem.at[j]).wait()
    bracket_copy(halo.at[mine], bracket).wait_send()
    far_copy.wait_send()
    seen_copy(theirs).wait_send()
    w_copy(mine).wait_send()
    for copy in mate_copies + face_copies:
        copy.wait_send()


def body(tiles, state, u, v, obs_index, obs_bin, obs_value, obs_weight, obs_blocks, loc_table):
    members, channels, rows, width = state.shape
    slots = obs_index.shape[1]
    half = rows // 2
    line = (channels, members, width)
    vmem = lambda *shape: pltpu.VMEM(shape, F32)
    dma = lambda n: pltpu.SemaphoreType.DMA((n,))
    anywhere = pl.BlockSpec(memory_space=pl.ANY)
    return pl.pallas_call(
        functools.partial(kernel, tiles),
        out_shape=pltpu.VMEM(state.shape, F32),
        in_specs=[anywhere] * 9,
        out_specs=anywhere,
        scratch_shapes=[
            vmem(LEVELS, 2 * rows, width),
            vmem(LEVELS, 2 * rows, width),
            pltpu.VMEM(obs_index.shape, jnp.int32),
            pltpu.VMEM(obs_bin.shape, jnp.int32),
            vmem(*obs_value.shape),
            vmem(*obs_weight.shape),
            pltpu.SMEM(obs_blocks.shape, jnp.int32),
            pltpu.SMEM(loc_table.shape, F32),
            vmem(rows + 3, *line),
            vmem(rows, *line),
            vmem(half, *line),
            vmem(2, *line),
            vmem(*line),
            vmem(rows + 2, *line),
            vmem(rows + 2, LEVELS, 5, 8, width),
            vmem(6, rows, slots),
            vmem(2, rows, slots),
            pltpu.VMEM((3, rows, slots), jnp.int32),
            vmem(half + 2, 2, 16, width),
            vmem(16, width),
            vmem(2, 16, width),
            vmem(2, 8, slots),
            vmem(members, slots),
            vmem(members, channels * width - slots),
            vmem(members, channels * width - slots),
            vmem(2, 2 * members, slots),
            vmem(2, 2 * members, slots),
            vmem(2, 2 * members, 128),
            vmem(2, 2 * members, 128),
            dma(rows), dma(LEVELS), dma(8), dma(4), dma(4), dma(4), dma(4), dma(half), dma(half), dma(half), dma(half),
            dma(2), dma(2), dma(2), dma(2), dma(2), dma(2), dma(half), dma(2),
        ],
        compiler_params=pltpu.CompilerParams(
            collective_id=0, has_side_effects=True, vmem_limit_bytes=56 * 1024 * 1024
        ),
        name="filter_cycle",
    )(state, u, v, obs_index, obs_bin, obs_value, obs_weight, obs_blocks, loc_table)


def solution(mesh):
    placed = (
        P("member", None, "tile", None),
        P(None, "tile", None),
        P(None, "tile", None),
        P("tile", None),
        P("tile", None),
        P("tile", None),
        P("tile", None),
        P("tile"),
        P(),
    )
    return jax.shard_map(
        functools.partial(body, mesh.shape["tile"]),
        mesh=mesh,
        in_specs=placed,
        out_specs=P("member", None, "tile", None),
        check_vma=False,
    )
```

```python
import functools

import jax
import jax.numpy as jnp
from jax import lax
from jax.experimental import pallas as pl
from jax.experimental.pallas import tpu as pltpu
from jax.sharding import PartitionSpec as P

BLOCK = 128
SWEEPS = 8
LEVELS = 4
MESH = pl.DeviceIdType.MESH
F32 = jnp.float32
highest = lax.Precision.HIGHEST


def mm(a, b, over):
    return lax.dot_general(
        a, b, (over, ((), ())), precision=highest, preferred_element_type=F32
    )


def inverse_root_weights(acc, total):
    row = lax.broadcasted_iota(jnp.int32, (total, total), 0)
    col = lax.broadcasted_iota(jnp.int32, (total, total), 1)
    eye = (row == col).astype(F32)
    smat = eye + acc[:, :total] * (1.0 / (total - 1))
    innov = acc[:, total : total + 1]
    scale = jnp.sqrt(jnp.sum(jnp.sum(smat * smat, axis=1, keepdims=True), axis=0, keepdims=True))
    ymat = smat / scale
    zmat = eye
    nn = ((1,), (0,))
    for sweep in range(SWEEPS):
        middle = 1.5 * eye - 0.5 * (ymat if sweep == 0 else mm(zmat, ymat, nn))
        if sweep < SWEEPS - 1:
            ymat = mm(ymat, middle, nn)
        zmat = middle if sweep == 0 else mm(middle, zmat, nn)
    inverse = mm(zmat, zmat, nn) / scale
    mean_weights = jnp.sum(inverse * innov, axis=0, keepdims=True) * (1.0 / (total - 1))
    return zmat.T / jnp.sqrt(scale) + mean_weights


def kernel(
    tiles,
    state, u_in, v_in, index_in, bin_in, value_in, weight_in, blocks_in, table_in,
    out,
    u, v, obs_index, obs_bin, obs_value, obs_weight, obs_blocks, loc_table,
    raw, bg, par, halo, bracket, once, coef, parts, hilo, dens, mean, place_of, dens_seen, split, near, far, chosen,
    seen, seen_par, wmat, wmat_send,
    load_sem, level_sem, in_sem, mate_ss, mate_rs, face_ss, face_rs, fwd_ss, fwd_rs, ret_ss, ret_rs,
    seen_ss, seen_rs, w_ss, w_rs, bracket_ss, bracket_rs, out_sem, edge_sem,
):
    members, channels, rows, width = state.shape
    half = rows // 2
    groups = members // 8
    total = 2 * members
    slots = index_in.shape[1]
    m, t = lax.axis_index("member"), lax.axis_index("tile")
    core = lax.rem(t, 2)
    sign = 1 - 2 * core
    first = core * (rows - 1)
    row_of = lambda e: first + sign * e
    is_edge = m == core
    partner = (1 - m, t)
    mate = (m, t + sign)
    facing = (1 - m, lax.rem(t - sign + tiles, tiles))
    rc = lambda src, dst, ss, rs, to: pltpu.make_async_remote_copy(
        src_ref=src, dst_ref=dst, send_sem=ss, recv_sem=rs, device_id=to, device_id_type=MESH
    )

    barrier = pltpu.get_barrier_semaphore()
    for peer in (partner, mate, facing):
        pl.semaphore_signal(barrier, inc=1, device_id=peer, device_id_type=MESH)

    fetch = lambda e, c, sem: pltpu.make_async_copy(
        state.at[:, c, row_of(e), :], raw.at[e + 1, c], sem
    )

    def load(e):
        @pl.loop(0, channels)
        def _(c):
            fetch(e, c, load_sem.at[e]).start()

    def loaded(e):
        pltpu.make_async_copy(raw.at[e + 1], raw.at[e + 1], load_sem.at[e]).wait()

    plain = [
        pltpu.make_async_copy(src, dst, in_sem.at[k])
        for k, (src, dst) in enumerate((
            (u_in, u.at[:, pl.ds(0, rows), :]), (v_in, v.at[:, pl.ds(0, rows), :]), (index_in, obs_index), (bin_in, obs_bin),
            (value_in, obs_value), (weight_in, obs_weight),
            (blocks_in, obs_blocks), (table_in, loc_table),
        ))
    ]
    start = jnp.where(is_edge, half, 2)
    others = [lax.rem(start + d, rows) for d in range(3, rows - 2)]
    for copy in plain[:2]:
        copy.start()

    @pl.loop(0, LEVELS)
    def _(level):
        @pl.loop(start - 2, start + 3)
        def _(e):
            for f in range(channels // LEVELS):
                fetch(e, f * LEVELS + level, level_sem.at[level]).start()

    mate_copies = [
        rc(raw.at[rows], raw.at[rows + 1], mate_ss.at[0], mate_rs.at[0], mate),
        rc(raw.at[rows - 1], raw.at[rows + 2], mate_ss.at[1], mate_rs.at[1], mate),
        rc(u_in.at[:, row_of(rows - 1), :], u.at[:, rows, :], mate_ss.at[2], mate_rs.at[2], mate),
        rc(v_in.at[:, row_of(rows - 1), :], v.at[:, rows, :], mate_ss.at[3], mate_rs.at[3], mate),
    ]
    face_copies = [
        rc(raw.at[1], halo.at[0], face_ss.at[0], face_rs.at[0], facing),
        rc(raw.at[2], halo.at[1], face_ss.at[1], face_rs.at[1], facing),
        rc(u_in.at[:, row_of(0), :], u.at[:, rows + 1, :], face_ss.at[2], face_rs.at[2], facing),
        rc(v_in.at[:, row_of(0), :], v.at[:, rows + 1, :], face_ss.at[3], face_rs.at[3], facing),
    ]
    sent_from = jnp.where(is_edge, half, 0)
    seen_copy = lambda j: rc(seen.at[j], seen_par.at[j], seen_ss.at[j], seen_rs.at[j], partner)
    w_copy = lambda j: rc(wmat_send.at[j], wmat.at[j], w_ss.at[j], w_rs.at[j], partner)
    bracket_copy = lambda src, dst: rc(src, dst, bracket_ss.at[0], bracket_rs.at[0], partner)
    far_copy = rc(chosen, far, bracket_ss.at[1], bracket_rs.at[1], partner)
    forward = lambda i: rc(bg.at[sent_from + i], par.at[i], fwd_ss.at[i], fwd_rs.at[i], partner)

    signf = sign.astype(F32)
    inner = t - sign
    at_rim = jnp.logical_or(inner < 0, inner >= tiles)
    keep = jnp.where(at_rim, 0.0, 1.0).astype(F32)

    def set_coef(e, level):
        r = jnp.where(e == rows, rows, jnp.where(e < 0, rows + 1, row_of(e)))
        cu, cv = u[level, pl.ds(r, 1), :] * signf, v[level, pl.ds(r, 1), :]
        up, um = jnp.maximum(cu, 0.0), jnp.maximum(-cu, 0.0)
        vp, vm = jnp.maximum(cv, 0.0), jnp.maximum(-cv, 0.0)
        inflow = up * jnp.where(e == 0, keep, 1.0)
        for k, term in enumerate((1.0 - up - um - vp - vm, inflow, um, vp, vm)):
            coef[e + 1, level, k] = jnp.broadcast_to(term, (8, width))

    lanes = 128
    parts_of_row = width // lanes
    lane = lax.broadcasted_iota(jnp.int32, (8, lanes), 1)

    def sweep_level(level, e, source, west, east, target):
        for p in range(parts_of_row):
            here, south, north = (
                pl.ds((p + d) % parts_of_row * lanes, lanes) for d in (0, parts_of_row - 1, 1)
            )
            term = [coef[e + 1, level, k, :, here] for k in range(5)]
            for c in range(channels // LEVELS):
                for g in range(groups):
                    at = lambda x: (c * LEVELS + level, pl.ds(g * 8, 8), x)
                    q = source[at(here)]
                    below = pltpu.roll(jnp.where(lane == lanes - 1, source[at(south)], q), 1, 1)
                    above = pltpu.roll(jnp.where(lane == 0, source[at(north)], q), lanes - 1, 1)
                    value = term[0] * q + term[3] * below + term[4] * above
                    if east is not None:
                        value = value + term[2] * east[at(here)]
                    if west is not None:
                        value = value + term[1] * west[at(here)]
                    target[at(here)] = value

    def sweep(*args):
        @pl.loop(0, LEVELS)
        def _(level):
            sweep_level(level, *args)

    def scale(e, k, source, target):
        @pl.loop(0, channels * groups)
        def _(i):
            c = i // groups
            here = pl.ds(pl.multiple_of(lax.rem(i, groups) * 8, 8), 8)
            target[c, here, :] = coef[e + 1, lax.rem(c, LEVELS), k] * source[c, here, :]

    step_one = lambda e: (e, raw.at[e + 1], raw.at[e], raw.at[e + 2], once.at[e + 1])
    step_two = lambda e: (e, once.at[e + 1], once.at[e], once.at[e + 2], bg.at[e])
    own_from = jnp.where(is_edge, 0, half)
    for copy in plain[:2]:
        copy.wait()

    @pl.loop(0, LEVELS)
    def _(level):
        some = raw.at[pl.ds(start - 1, 5), pl.ds(0, channels // LEVELS)]
        pltpu.make_async_copy(some, some, level_sem.at[level]).wait()

        @pl.loop(start - 1, start + 2)
        def _(e):
            set_coef(e, level)
            sweep_level(level, *step_one(e))

        sweep_level(level, *step_two(start))
        i = start - sent_from

        @pl.when(level == 0)
        def _():
            pl.semaphore_wait(barrier, 3)

        for f in range(channels // LEVELS):
            c = f * LEVELS + level
            rc(bg.at[start, c], par.at[i, c], fwd_ss.at[i], fwd_rs.at[i], partner).start()

        @pl.when(level == 0)
        def _():
            for e in others:
                load(e)
            for copy in plain[2:]:
                copy.start()

    for e in others:
        loaded(e)
    for copy in mate_copies + face_copies[2:] + face_copies[:2]:
        copy.start()
    raw[0] = jnp.zeros(raw.shape[1:], F32)

    ahead = rows - 1 - start

    @pl.loop(0, rows - 2)
    def _(k):
        up = k < ahead
        e = jnp.where(up, start + 1 + k, start - 1 - (k - ahead))
        new = jnp.where(up, e + 1, e - 1)

        @pl.when(new == rows - 1)
        def _():
            for copy in mate_copies:
                copy.wait_recv()

        @pl.loop(0, LEVELS)
        def _(level):
            set_coef(new, level)
            sweep_level(level, *step_one(new))
            sweep_level(level, *step_two(e))

        @pl.when(jnp.where(is_edge, e >= half, jnp.logical_and(e >= 2, e < half)))
        def _():
            forward(e - sent_from).start()

    for copy in face_copies[2:]:
        copy.wait_recv()

    @pl.loop(0, LEVELS)
    def _(level):
        set_coef(-1, level)

    scale(-1, 2, raw.at[1], once.at[0])
    sweep(*step_two(0))

    for copy in plain[2:]:
        copy.wait()
    bins = obs_bin[...]
    local = jnp.zeros((rows, slots), F32)
    for b in range(loc_table.shape[0]):
        local = jnp.where(bins == b, loc_table[b], local)
    row_id = lax.broadcasted_iota(jnp.int32, (rows, slots), 0)
    live = jnp.zeros((rows, slots), jnp.int32)
    for r in range(rows):
        live = jnp.where(row_id == r, obs_blocks[r] * BLOCK, live)
    slot_id = lax.broadcasted_iota(jnp.int32, (rows, slots), 1)
    weight = jnp.where(slot_id < live, obs_weight[...] * local, 0.0)
    for k, term in enumerate((weight, weight * obs_value[...])):
        for piece in range(3):
            head = term.astype(jnp.bfloat16).astype(F32)
            parts[3 * k + piece] = head
            term = term - head
    index = obs_index[...]
    hilo[0] = ((index >> 7) & 3) * 16 + (index >> 9)
    hilo[1] = index & 127
    hilo[2] = index
    chunk = 512

    by_channel = lambda x: jnp.concatenate([x[16 * q : 16 * q + 16] for q in range(4)], axis=1)

    @pl.loop(jnp.where(is_edge, 2, 0), half + 2)
    def _(k):
        r = pl.ds(row_of(jnp.where(k < half, own_from + k, k - half)), 1)

        def add(j, acc):
            at = pl.ds(pl.multiple_of(j * chunk, chunk), chunk)
            high = lax.broadcasted_iota(jnp.int32, (64, chunk), 0) == hilo[0, r, at]
            low = lax.broadcasted_iota(jnp.int32, (128, chunk), 0) == hilo[1, r, at]
            left = jnp.concatenate(
                [jnp.where(high, parts[p, r, at], 0.0).astype(jnp.bfloat16) for p in range(6)]
                + [jnp.where(high, 1.0, 0.0).astype(jnp.bfloat16)],
                axis=0,
            )
            right = jnp.where(low, 1.0, 0.0).astype(jnp.bfloat16)
            return acc + lax.dot_general(
                left, right, (((1,), (1,)), ((), ())), preferred_element_type=F32
            )

        acc = lax.fori_loop(0, slots // chunk, add, jnp.zeros((448, 128), F32))
        for p in range(2):
            whole = acc[192 * p : 192 * p + 64]
            whole = whole + acc[192 * p + 64 : 192 * p + 128]
            whole = whole + acc[192 * p + 128 : 192 * p + 192]
            dens[k, p] = by_channel(whole)

        @pl.when(k >= half)
        def _():
            hit = jnp.where(acc[384:] > 0.0, 1.0, 0.0)
            iota = lambda shape, d: lax.broadcasted_iota(jnp.int32, shape, d)
            order = lambda x: (x & 15) * 4 + (x >> 4)
            square, lines = (128, 128), (64, 64)
            left_of = jnp.where(iota(square, 0) < iota(square, 1), 1.0, 0.0).astype(jnp.bfloat16)
            above = jnp.where(order(iota(lines, 1)) < order(iota(lines, 0)), 1.0, 0.0)
            count = jnp.broadcast_to(jnp.sum(hit, axis=1, keepdims=True), hit.shape)
            exact = lambda x, y: lax.dot_general(
                x.astype(jnp.bfloat16), y.astype(jnp.bfloat16),
                (((1,), (0,)), ((), ())), preferred_element_type=F32,
            )
            rank = exact(hit, left_of) + exact(above, count)
            entry = (order(iota(hit.shape, 0)) * 128 + iota(hit.shape, 1)).astype(F32)
            seen_count = jnp.sum(count[:, :1], axis=0, keepdims=True)
            place_of[k - half] = by_channel(
                jnp.where(hit > 0.0, rank, seen_count + entry - rank)
            ).astype(jnp.int32)

    mine = jnp.where(is_edge, 0, 1)
    theirs = 1 - mine

    def pieces_of(x):
        pieces = []
        for _ in range(3):
            pieces.append(x.astype(jnp.bfloat16))
            x = x - pieces[-1].astype(F32)
        return jnp.concatenate(pieces, axis=0)

    def thirds(x):
        n = x.shape[0] // 3
        return x[:n] + x[n : 2 * n] + x[2 * n :]

    def hot(j, c, part):
        n = lax.broadcasted_iota(jnp.int32, (chunk, width), 0)
        place = place_of[j, pl.ds(c, 1), :] - part * chunk
        return jnp.where(n == place, 1.0, 0.0).astype(jnp.bfloat16)

    def pick(left, right, over):
        return thirds(
            lax.dot_general(left, right, (over, ((), ())), preferred_element_type=F32)
        )

    def look():
        for copy in face_copies[:2]:
            copy.wait_recv()
        sweep(-1, halo.at[0], halo.at[1], None, once.at[0])
        scale(0, 1, halo.at[0], once.at[1])
        sweep(0, once.at[1], once.at[0], None, halo.at[0])
        scale(1, 1, once.at[1], halo.at[1])

        @pl.loop(0, 2)
        def _(n):
            j = jnp.where(n == 0, theirs, mine)
            seen[j] = jnp.zeros((total, slots), F32)
            dens_seen[j] = jnp.zeros((8, slots), F32)

            @pl.loop(0, channels)
            def _(c):
                here = pl.ds(c, 1)
                blank = jnp.zeros((6, width), F32)
                left = pieces_of(
                    jnp.concatenate(
                        [bg[j, c], halo[j, c], dens[half + j, 0, here, :], dens[half + j, 1, here, :], blank],
                        axis=0,
                    )
                )
                for part in range(slots // chunk):
                    at = pl.ds(part * chunk, chunk)
                    found = pick(left, hot(j, c, part), ((1,), (1,)))
                    seen[j, :, at] += found[:total]
                    dens_seen[j, :, at] += found[total:]

            @pl.when(n == 0)
            def _():
                seen_copy(j).start()

    def add(x, density, departure, acc):
        middle = jnp.sum(x, axis=0, keepdims=True) * (1.0 / total)
        x = x - middle
        departure = departure - density * middle
        right = jnp.concatenate([x * density, jnp.broadcast_to(departure, (8, width))], axis=0)
        return middle, acc + mm(x, right, ((1,), (1,)))

    nothing = jnp.zeros((total, total + 8), F32)

    def spread(j):
        weights = wmat[j, :, :total]

        @pl.loop(0, channels)
        def _(c):
            x = mm(weights, jnp.concatenate([bg[j, c], halo[j, c]], axis=0), ((1,), (0,)))
            bg[j, c] = x[:members]
            halo[j, c] = x[members:]

            @pl.when(j == mine)
            def _():
                bracket_copy(halo.at[j, c], bracket.at[c]).start()

    def lead(j):
        seen_copy(j).wait_recv()

        def columns(n, acc):
            at = pl.ds(pl.multiple_of(n * width, width), width)
            x = jnp.concatenate(
                [
                    seen[j, :members, at] + seen_par[j, members:, at],
                    seen[j, members:, at] + seen_par[j, :members, at],
                ],
                axis=0,
            )
            return add(x, dens_seen[j, 0:1, at], dens_seen[j, 1:2, at], acc)[1]

        weights = inverse_root_weights(lax.fori_loop(0, slots // width, columns, nothing), total)
        weights = weights + (1.0 - jnp.sum(weights, axis=1, keepdims=True)) * (1.0 / total)
        wmat[j, :, :total] = weights
        turned = jnp.concatenate([weights[members:], weights[:members]], axis=0)
        wmat_send[j, :, :total] = jnp.concatenate(
            [turned[:, members:], turned[:, :members]], axis=1
        )
        w_copy(j).start()
        for part in range(slots // chunk):
            at = pl.ds(part * chunk, chunk)
            x = jnp.concatenate([seen_par[j, members:, at], seen_par[j, :members, at]], axis=0)
            near[:, at] = mm(weights[:members], x, ((1,), (0,)))

    def choose(j):
        chosen[...] = jnp.zeros(chosen.shape, F32)

        @pl.loop(0, channels)
        def _(c):
            left = pieces_of(halo[j, c])
            for part in range(chosen.shape[1] // chunk):
                at = pl.ds(part * chunk, chunk)
                chosen[:, at] += pick(left, hot(j, c, part + slots // chunk), ((1,), (1,)))

        far_copy.start()

    def split_share(source, first):
        for part in range(source.shape[1] // chunk):
            at = pl.ds(part * chunk, chunk)
            split[:, pl.ds((first + part) * chunk, chunk)] = pieces_of(source[:, at])

    def gather_back(j, c, first, last):
        share = jnp.zeros((members, width), F32)
        for part in range(first, last):
            left = split[:, pl.ds(part * chunk, chunk)]
            share = share + pick(left, hot(j, c, part), ((1,), (0,)))
        return share

    known = slots // chunk

    def add_near():
        split_share(near, 0)

        @pl.loop(0, channels)
        def _(c):
            bg[mine, c] += gather_back(mine, c, 0, known)

    @pl.loop(0, half)
    def _(k):
        i = jnp.where(is_edge, 2 + k // (half - 1), k)
        e = own_from + i

        @pl.when(k == jnp.where(is_edge, 0, 1))
        def _():
            look()

        @pl.when(k == half - 2)
        def _():
            lead(mine)

        @pl.when(jnp.logical_and(is_edge, k == half - 1))
        def _():
            add_near()

        @pl.when(k == half - 1)
        def _():
            w_copy(theirs).wait_recv()

        @pl.when(k >= half - 2)
        def _():
            spread(jnp.where(k == half - 2, mine, theirs))

        @pl.when(k == half - 1)
        def _():
            choose(theirs)

        @pl.when(jnp.logical_or(jnp.logical_not(is_edge), lax.rem(k, half - 1) == 0))
        def _():
            forward(i).wait_recv()

            def both(c):
                return jnp.concatenate([bg[e, c], par[i, c]], axis=0)

            def column(c, acc):
                here = pl.ds(c, 1)
                middle, acc = add(both(c), dens[i, 0, here, :], dens[i, 1, here, :], acc)
                mean[here, :] = middle
                return acc

            weights = inverse_root_weights(lax.fori_loop(0, channels, column, nothing), total)

            @pl.loop(0, channels)
            def _(c):
                middle = mean[pl.ds(c, 1), :]
                x = middle + mm(weights, both(c) - middle, ((1,), (0,)))
                bg[e, c] = x[:members]
                par[i, c] = x[members:]
                place = out.at[:, c, row_of(e), :]
                rc(par.at[i, c], place, ret_ss.at[i], ret_rs.at[i], partner).start()
                pltpu.make_async_copy(bg.at[e, c], place, out_sem.at[i]).start()

    def finish(j, share):
        @pl.loop(0, channels)
        def _(c):
            bg[j, c] += share(c)
            pltpu.make_async_copy(bg.at[j, c], out.at[:, c, row_of(j), :], edge_sem.at[j]).start()

    @pl.when(jnp.logical_not(is_edge))
    def _():
        add_near()

    bracket_copy(halo.at[mine], bracket).wait_recv()
    finish(theirs, lambda c: bracket[c])
    far_copy.wait_recv()
    split_share(far, known)
    finish(mine, lambda c: gather_back(mine, c, known, channels * width // chunk))

    back = lambda i: rc(
        par.at[i], out.at[:, :, row_of(sent_from + i), :], ret_ss.at[i], ret_rs.at[i], partner
    )

    def direct(i):
        pltpu.make_async_copy(bg.at[own_from + i], bg.at[own_from + i], out_sem.at[i]).wait()
        back(i).wait_send()

    @pl.when(is_edge)
    def _():
        for i in range(2, half):
            direct(i)
        for i in range(half):
            back(i).wait_recv()
            forward(i).wait_send()

    @pl.when(jnp.logical_not(is_edge))
    def _():
        for i in range(half):
            direct(i)
        for i in range(2, half):
            back(i).wait_recv()
            forward(i).wait_send()

    for j in range(2):
        pltpu.make_async_copy(bg.at[j], bg.at[j], edge_sem.at[j]).wait()
    bracket_copy(halo.at[mine], bracket).wait_send()
    far_copy.wait_send()
    seen_copy(theirs).wait_send()
    w_copy(mine).wait_send()
    for copy in mate_copies + face_copies:
        copy.wait_send()


def body(tiles, state, u, v, obs_index, obs_bin, obs_value, obs_weight, obs_blocks, loc_table):
    members, channels, rows, width = state.shape
    slots = obs_index.shape[1]
    half = rows // 2
    line = (channels, members, width)
    vmem = lambda *shape: pltpu.VMEM(shape, F32)
    dma = lambda n: pltpu.SemaphoreType.DMA((n,))
    anywhere = pl.BlockSpec(memory_space=pl.ANY)
    return pl.pallas_call(
        functools.partial(kernel, tiles),
        out_shape=pltpu.VMEM(state.shape, F32),
        in_specs=[anywhere] * 9,
        out_specs=anywhere,
        scratch_shapes=[
            vmem(LEVELS, 2 * rows, width),
            vmem(LEVELS, 2 * rows, width),
            pltpu.VMEM(obs_index.shape, jnp.int32),
            pltpu.VMEM(obs_bin.shape, jnp.int32),
            vmem(*obs_value.shape),
            vmem(*obs_weight.shape),
            pltpu.SMEM(obs_blocks.shape, jnp.int32),
            pltpu.SMEM(loc_table.shape, F32),
            vmem(rows + 3, *line),
            vmem(rows, *line),
            vmem(half, *line),
            vmem(2, *line),
            vmem(*line),
            vmem(rows + 2, *line),
            vmem(rows + 2, LEVELS, 5, 8, width),
            vmem(6, rows, slots),
            pltpu.VMEM((3, rows, slots), jnp.int32),
            vmem(half + 2, 2, 16, width),
            vmem(16, width),
            pltpu.VMEM((2, 16, width), jnp.int32),
            vmem(2, 8, slots),
            pltpu.VMEM((3 * members, channels * width), jnp.bfloat16),
            vmem(members, slots),
            vmem(members, channels * width - slots),
            vmem(members, channels * width - slots),
            vmem(2, 2 * members, slots),
            vmem(2, 2 * members, slots),
            vmem(2, 2 * members, 128),
            vmem(2, 2 * members, 128),
            dma(rows), dma(LEVELS), dma(8), dma(4), dma(4), dma(4), dma(4), dma(half), dma(half), dma(half), dma(half),
            dma(2), dma(2), dma(2), dma(2), dma(2), dma(2), dma(half), dma(2),
        ],
        compiler_params=pltpu.CompilerParams(
            collective_id=0, has_side_effects=True, vmem_limit_bytes=56 * 1024 * 1024
        ),
        name="filter_cycle",
    )(state, u, v, obs_index, obs_bin, obs_value, obs_weight, obs_blocks, loc_table)


def solution(mesh):
    placed = (
        P("member", None, "tile", None),
        P(None, "tile", None),
        P(None, "tile", None),
        P("tile", None),
        P("tile", None),
        P("tile", None),
        P("tile", None),
        P("tile"),
        P(),
    )
    return jax.shard_map(
        functools.partial(body, mesh.shape["tile"]),
        mesh=mesh,
        in_specs=placed,
        out_specs=P("member", None, "tile", None),
        check_vma=False,
    )
```
